32 devices in a mesh: dp: 8 (over z, y), tensor: 4 (over x, core).
Axes of the slice: x: 2, y: 2, z: 4, core: 2. Of those that a mesh axis runs over, the one named last changes fastest.
Arguments:
- tokens: bfloat16 [4096, 768], P('dp'), may hold values from -6 to 6
- lengths: int32 [8, 3], P('dp'), may hold values from 1 to 384, 512 in all within a row
- routes: int32 [4096, 2], P('dp'), may hold values from 0 to 63, all different within a row; in each aligned block of 512 rows (0 to 511, 512 to 1023, ...) at most 32 rows name the same one
- rel_bucket: int32 [384], replicated, may hold values from 0 to 31, as said below
- norm1: bfloat16 [768], replicated, may hold values from 0.5 to 1.5
- w_query: bfloat16 [768, 768], P(None, 'tensor'), may hold values from -0.21875 to 0.21875
- w_key: bfloat16 [768, 768], P(None, 'tensor'), may hold values from -0.21875 to 0.21875
- w_value: bfloat16 [768, 768], P(None, 'tensor'), may hold values from -0.21875 to 0.21875
- output_weight: bfloat16 [768, 768], P('tensor'), may hold values from -1.75 to 1.75
- position_bias_table: bfloat16 [12, 32], P('tensor'), may hold values from -4 to 4
- norm2: bfloat16 [768], replicated, may hold values from 0.5 to 1.5
- router: bfloat16 [768, 64], replicated, may hold values from -0.14941406 to 0.14941406
- expert_in: bfloat16 [64, 768, 3072], P('dp', None, 'tensor'), may hold values from -0.21875 to 0.21875
- expert_out: bfloat16 [64, 3072, 768], P('dp', 'tensor'), may hold values from -0.109375 to 0.109375
- cotangent: bfloat16 [4096, 768], P('dp'), may hold values from -6 to 6
Outputs:
- layer_out: bfloat16 [4096, 768], P('dp')
- grad_tokens: float32 [4096, 768], P('dp')
- grad_norm1: float32 [768], replicated
- grad_query: float32 [768, 768], P(None, 'tensor')
- grad_key: float32 [768, 768], P(None, 'tensor')
- grad_value: float32 [768, 768], P(None, 'tensor')
- grad_output: float32 [768, 768], P('tensor')
- gradient_bias_table: float32 [12, 32], P('tensor')
- grad_norm2: float32 [768], replicated
- grad_router: float32 [768, 64], replicated
- grad_expert_in: float32 [64, 768, 3072], P('dp', None, 'tensor')
- grad_expert_out: float32 [64, 3072, 768], P('dp', 'tensor')
The draws below stay inside these ranges and needn't reach their ends.
Inputs may be any that keep to these rules, and one draw needn't show every extreme that they name: `lengths`: each row sums to 512 and its largest entry is 384. `routes`: a token names 2 different experts; among the tokens of one index of dp no expert is named more than 32 times, a bound that some block reaches. `rel_bucket`: nondecreasing in the offset; offsets below 16 are their own bucket; the last offset has bucket 32 - 1.
All inputs are finite; a program needn't handle non-finite values.
Results may differ from the reference program's by a relative error of at most 0.017.
Values may be sent and summed in bfloat16 or wider, within the bound.
No kernel may reach another device: no remote copies, remote signals or barrier semaphores. Data moves between devices by JAX's collectives and lax.ppermute only.
A program may use at most 192 MiB of HBM per device.

```python
import math
import jax
import jax.numpy as jnp
import numpy as np
from jax import lax

D = 768
HEADS = 12
HEAD_DIM = 64
FF = 3072
EXPERTS = 64
TOP = 2
BUCKETS = 32
SEQ_DEV = 3
TOK_DEV = 512
GROUPS = 8
TOKENS = 4096
SEQ_MAX = 384
CAP = 32


def draw_rel_bucket(key, part):
    key = jax.random.fold_in(key, 7)
    half_point = BUCKETS // 2
    offsets = jnp.arange(SEQ_MAX, dtype=jnp.int32)
    strides = jax.random.randint(key, (SEQ_MAX,), 1, 4, dtype=jnp.int32)
    climbs = jnp.cumsum(jnp.where(offsets > half_point, strides, 0))
    far_bucket = half_point + climbs * (BUCKETS - 1 - half_point) // climbs[SEQ_MAX - 1]
    return jnp.where(offsets < half_point, offsets, far_bucket).astype(jnp.int32)


def levels(rng, dims, cuts, low, high):
    def one(position, parts):
        heights = jax.random.uniform(jax.random.fold_in(jax.random.fold_in(rng, 6), position), (parts,), jnp.float32, low / len(cuts), high / len(cuts))
        return jnp.repeat(jnp.exp(heights), dims[position] // parts).reshape((-1,) + (1,) * (len(dims) - position - 1))

    factor_of = one(*cuts[0])
    for cut in cuts[1:]:
        factor_of = factor_of * one(*cut)
    return factor_of


def length_profile(amount, total, reach, slope):
    weights = [(1 << 20) // math.isqrt(standing ** slope) + 1 for standing in range(2, amount + 1)]
    spare, given = total - reach - (amount - 1), [1] * (amount - 1)
    while spare > 0:
        movable = [i for i in range(amount - 1) if given[i] < reach]
        pool, budget = sum([weights[i] for i in movable]), spare
        for i in movable:
            addition = min(reach - given[i], max(1, budget * weights[i] // pool), spare)
            given[i] = given[i] + addition
            spare = spare - addition
    return np.array([reach] + given)


def ragged(key, number_of, total, bound, slope):
    if number_of == 2:
        one = jax.random.randint(key, (), max(1, total - bound), min(bound, total - 1) + 1)
        return jnp.stack([one, total - one])
    tallies = jnp.asarray(length_profile(number_of, total, bound, slope), jnp.int32)
    pairs = (number_of - 1) // 2
    donor, receiver = tallies[1:1 + 2 * pairs:2], tallies[2:2 + 2 * pairs:2]
    margin = jnp.minimum(donor - 1, bound - receiver)
    moved = jax.random.randint(jax.random.fold_in(key, 1), (pairs,), 0, 1 << 20) % (margin + 1)
    tallies = tallies.at[1:1 + 2 * pairs:2].set(donor - moved).at[2:2 + 2 * pairs:2].set(receiver + moved)
    return tallies[jax.random.permutation(jax.random.fold_in(key, 2), number_of)]


def assign_block(key, own, number, rows, number_of, top, limit, skew):
    order = jax.random.permutation(key, number_of)
    packed, usual = shares(number_of, rows * top, limit, skew, True), shares(number_of, rows * top, limit, skew, False)
    places = jnp.arange(number_of)

    def named(tallies, turn):
        used = int((tallies > 0).sum())
        fixed = max(1, used // 4)
        passed = fixed + (places - fixed + turn * (used - fixed)) % max(1, number_of - fixed)
        return jnp.zeros((number_of,), jnp.int32).at[order[jnp.where(places < fixed, places, passed)]].set(jnp.asarray(tallies, jnp.int32))

    tallies = jnp.where(number % 4 == 0, named(packed, number // 4), named(usual, number - number // 4 - 1))
    mixed = jax.random.permutation(jax.random.fold_in(own, 3), number_of)
    donor, receiver = mixed[0:number_of // 2 * 2:2], mixed[1:number_of // 2 * 2:2]
    room = jnp.minimum(tallies[donor] - 1, limit - tallies[receiver]) // 2
    room = jnp.where((donor == order[0]) | (receiver == order[0]) | (tallies[receiver] == 0), 0, jnp.maximum(room, 0))
    passed = jax.random.randint(jax.random.fold_in(own, 4), (number_of // 2,), 0, 1 << 20) % (room + 1)
    tallies = tallies.at[donor].add(-passed).at[receiver].add(passed)
    labels = jnp.searchsorted(jnp.cumsum(tallies), jnp.arange(rows * top), side="right").astype(jnp.int32)
    listing = labels.reshape(top, rows).T
    listing = listing[jax.random.permutation(jax.random.fold_in(own, 1), rows)]
    turn = jax.random.randint(jax.random.fold_in(own, 2), (rows, 1), 0, top)
    return jnp.take_along_axis(listing, (jnp.arange(top)[None, :] + turn) % top, axis=1)


def shares(amount, total, reach, slope, full):
    portions = [(1 << 20) // math.isqrt(grade ** slope) + 1 for grade in range(1, amount + 1)]
    largest = reach if full else min(reach, max(-(-total // amount), total * portions[0] // sum(portions)))
    least = 1 if total - largest >= amount - 1 else 0
    holding, spare = [largest] + [least] * (amount - 1), total - largest - least * (amount - 1)
    while spare > 0:
        free = [i for i in range(1, amount) if holding[i] < largest] or [i for i in range(1, amount) if holding[i] < reach]
        whole, remaining = sum([portions[i] for i in free]), spare
        for i in free:
            extra = min(reach - holding[i], max(1, remaining * portions[i] // whole), spare)
            holding[i] = holding[i] + extra
            spare = spare - extra
    return np.array(holding)


def normal_values(stream_key, shape, spread, reach, shards=(), held_as=jnp.bfloat16):
    level = levels(stream_key, shape, shards, -0.22, 0.18) if shards else 1.0
    array = jax.random.normal(stream_key, shape, jnp.float32) * spread * level
    return jnp.minimum(jnp.maximum(array, -reach), reach).astype(held_as)


def setup_inputs(seed: int = 0) -> dict:
    arg_keys = jax.random.split(jax.random.key(seed), 16)
    tokens = normal_values(arg_keys[0], (TOKENS, D), 1.0, 6.0, ((0, 8),))
    lengths = jax.vmap(lambda own: ragged(own, SEQ_DEV, TOK_DEV, SEQ_MAX, 2))(jax.random.split(arg_keys[1], GROUPS)).reshape((GROUPS, SEQ_DEV)).astype(jnp.int32)
    routes_keys = jax.random.split(jax.random.fold_in(arg_keys[2], 1), TOKENS // TOK_DEV)
    routes_turns = jax.random.permutation(jax.random.fold_in(arg_keys[2], 3), TOKENS // TOK_DEV)
    routes = jax.vmap(lambda own, number: assign_block(jax.random.fold_in(arg_keys[2], 2), own, number, TOK_DEV, EXPERTS, TOP, CAP, 2))(routes_keys, routes_turns).reshape((TOKENS, TOP))
    rel_bucket = draw_rel_bucket(jax.random.fold_in(arg_keys[15], 71), 0)
    norm1 = jnp.clip(1.0 + 0.1 * jax.random.normal(arg_keys[4], (D,), jnp.float32), 0.5, 1.5).astype(jnp.bfloat16)
    w_query = normal_values(arg_keys[5], (D, HEADS * HEAD_DIM), D ** -0.5, 0.21875, ((1, 4),))
    w_key = normal_values(arg_keys[6], (D, HEADS * HEAD_DIM), D ** -0.5, 0.21875, ((1, 4),))
    w_value = normal_values(arg_keys[7], (D, HEADS * HEAD_DIM), D ** -0.5, 0.21875, ((1, 4),))
    output_weight = normal_values(arg_keys[8], (HEADS * HEAD_DIM, D), (HEADS * HEAD_DIM // 64) ** -0.5, 1.75, ((0, 4),))
    position_bias_table = normal_values(arg_keys[9], (HEADS, BUCKETS), 1.0, 4.0, ((0, 4),))
    norm2 = jnp.clip(1.0 + 0.1 * jax.random.normal(arg_keys[10], (D,), jnp.float32), 0.5, 1.5).astype(jnp.bfloat16)
    router = normal_values(arg_keys[11], (D, EXPERTS), 0.025, 0.14941406)
    expert_in = normal_values(arg_keys[12], (EXPERTS, D, FF), D ** -0.5, 0.21875, ((0, 8), (2, 4)))
    expert_out = normal_values(arg_keys[13], (EXPERTS, FF, D), FF ** -0.5, 0.109375, ((0, 8), (1, 4)))
    cotangent = normal_values(arg_keys[14], (TOKENS, D), 1.0, 6.0, ((0, 8),))
    return dict(tokens=tokens, lengths=lengths, routes=routes, rel_bucket=rel_bucket, norm1=norm1, w_query=w_query, w_key=w_key, w_value=w_value, output_weight=output_weight, position_bias_table=position_bias_table, norm2=norm2, router=router, expert_in=expert_in, expert_out=expert_out, cotangent=cotangent)


@jax.custom_vjp
def low(v):
    return lax.optimization_barrier(v.astype(jnp.bfloat16)).astype(jnp.float32)

@jax.custom_vjp
def low_back(v):
    return v

def low_keep(v):
    return (low(v), None)

def lower_precision_pass(kept, grad):
    return (grad,)

def back_keep(v):
    return (v, None)

def back_low(kept, grad):
    return (low(grad),)
low.defvjp(low_keep, lower_precision_pass)
low_back.defvjp(back_keep, back_low)
highest = lax.Precision.HIGHEST
epsilon = 1e-06

def rms_norm(values, gain):
    return values * lax.rsqrt(lax.optimization_barrier(jnp.mean(values * values, axis=-1, keepdims=True)) + epsilon) * gain

def segment_ids(lengths_row):
    seq_ends = jnp.cumsum(lengths_row)
    positions = jnp.arange(TOK_DEV, dtype=jnp.int32)
    return lax.optimization_barrier(jnp.sum((positions[:, None] >= seq_ends[None, :]).astype(jnp.int32), axis=1))

def route_slots(routes):
    per_group = routes.reshape(GROUPS, TOK_DEV * TOP)
    route_hits = (per_group[:, :, None] == jnp.arange(EXPERTS, dtype=jnp.int32)).astype(jnp.int32)
    slot_rank = jnp.cumsum(route_hits, axis=1) - 1
    return lax.optimization_barrier(jnp.sum(slot_rank * route_hits, axis=2)).reshape(TOKENS, TOP)

def attention_device(inputs, segment, norm1, w_query, w_key, w_value, output_weight, position_bias_table, rel_bucket):
    normed = low(rms_norm(inputs, norm1))
    query_heads = low(low_back(jnp.dot(normed, w_query, precision=highest))).reshape(TOK_DEV, HEADS, HEAD_DIM)
    key_heads = low(low_back(jnp.dot(normed, w_key, precision=highest))).reshape(TOK_DEV, HEADS, HEAD_DIM)
    value_heads = low(low_back(jnp.dot(normed, w_value, precision=highest))).reshape(TOK_DEV, HEADS, HEAD_DIM)
    row_count = min(512, TOK_DEV)
    score_scale = HEAD_DIM ** (-0.5)
    key_index = jnp.arange(TOK_DEV, dtype=jnp.int32)

    def one_block(row_start):
        query_block = lax.dynamic_slice_in_dim(query_heads, row_start, row_count, 0)
        query_index = row_start + jnp.arange(row_count, dtype=jnp.int32)
        offset = jnp.clip(query_index[:, None] - key_index[None, :], 0, SEQ_MAX - 1)
        scores = jnp.einsum('qhd,khd->hqk', query_block, key_heads, precision=highest) * score_scale
        scores = low_back(scores + position_bias_table[:, rel_bucket[offset]])
        segment_block = lax.dynamic_slice_in_dim(segment, row_start, row_count, 0)
        allowed = (segment_block[:, None] == segment[None, :]) & (query_index[:, None] >= key_index[None, :])
        scores = jnp.where(allowed[None], scores, -1e+30)
        lifted = jnp.exp(scores - lax.optimization_barrier(jnp.max(scores, axis=2, keepdims=True)))
        weights = low(lifted / lax.optimization_barrier(jnp.sum(lifted, axis=2, keepdims=True)))
        return jnp.einsum('hqk,khd->qhd', weights, value_heads, precision=highest)
    starts = jnp.arange(TOK_DEV // row_count, dtype=jnp.int32) * row_count
    attended = lax.map(jax.checkpoint(one_block), starts).reshape(TOK_DEV, HEADS * HEAD_DIM)
    attended = low(low_back(attended))
    branch = low_back(jnp.dot(attended, output_weight, precision=highest))
    return inputs + branch

def forward(tokens, norm1, w_query, w_key, w_value, output_weight, position_bias_table, norm2, router, expert_in, expert_out, segments, routes, columns, gather_index, rel_bucket):
    groups = tokens.reshape(GROUPS, TOK_DEV, D)

    def group_layer(pair_in):
        return attention_device(pair_in[0], pair_in[1], norm1, w_query, w_key, w_value, output_weight, position_bias_table, rel_bucket)
    hidden_state = lax.map(jax.checkpoint(group_layer), (groups, segments)).reshape(TOKENS, D)
    normed = low(rms_norm(hidden_state, norm2))
    logits = jnp.dot(normed, router, precision=highest)
    chosen = jnp.take_along_axis(logits, routes, axis=1)
    gate_weights = jax.nn.softmax(chosen, axis=1)
    padded = jnp.concatenate([normed, jnp.zeros((1, D), jnp.float32)], axis=0)

    def one_expert(expert_inputs):
        weight_first, weight_second, index_row = expert_inputs
        rows_in = padded[index_row]
        pre_gelu = low_back(jnp.dot(rows_in, weight_first, precision=highest))
        activated = low(jax.nn.gelu(pre_gelu, approximate=True))
        return jnp.dot(activated, weight_second, precision=highest)
    expert_all = lax.map(jax.checkpoint(one_expert), (expert_in, expert_out, gather_index))
    expert_rows = low_back(expert_all[routes, columns])
    return hidden_state + lax.optimization_barrier(jnp.sum(gate_weights[:, :, None] * expert_rows, axis=1))

def reference(tokens, lengths, routes, rel_bucket, norm1, w_query, w_key, w_value, output_weight, position_bias_table, norm2, router, expert_in, expert_out, cotangent):
    segments = jax.vmap(segment_ids)(lengths)
    slot_index = route_slots(routes)
    group_of = jnp.arange(TOKENS, dtype=jnp.int32) // TOK_DEV
    columns = group_of[:, None] * CAP + slot_index
    token_ids = jnp.broadcast_to(jnp.arange(TOKENS, dtype=jnp.int32)[:, None], (TOKENS, TOP))
    gather_index = jnp.full((EXPERTS, GROUPS * CAP), TOKENS, jnp.int32).at[routes, columns].set(token_ids)

    def layer(tokens_f, norm1_f, query_f, key_f, value_f, output_f, table_f, norm2_f, router_f, first_f, second_f):
        return forward(tokens_f, norm1_f, query_f, key_f, value_f, output_f, table_f, norm2_f, router_f, first_f, second_f, segments, routes, columns, gather_index, rel_bucket)
    floats = [tokens.astype(jnp.float32), norm1.astype(jnp.float32), w_query.astype(jnp.float32), w_key.astype(jnp.float32), w_value.astype(jnp.float32), output_weight.astype(jnp.float32), position_bias_table.astype(jnp.float32), norm2.astype(jnp.float32), router.astype(jnp.float32), expert_in.astype(jnp.float32), expert_out.astype(jnp.float32)]
    result, pullback = jax.vjp(layer, *floats)
    gradients = pullback(cotangent.astype(jnp.float32))
    return (result.astype(jnp.bfloat16), gradients[0], gradients[1], gradients[2], gradients[3], gradients[4], gradients[5], gradients[6], gradients[7], gradients[8], gradients[9], gradients[10])
```

```python
import jax
import jax.numpy as jnp
from jax import lax
from jax.sharding import PartitionSpec as P

epsilon = 1e-06
masked_value = -1e30


def segment_ids(lengths_row, token_count):
    seq_ends = jnp.cumsum(lengths_row)
    positions = jnp.arange(token_count, dtype=jnp.int32)
    return jnp.sum((positions[:, None] >= seq_ends[None, :]).astype(jnp.int32), axis=1)


def route_slots(routes, experts):
    flat_routes = routes.reshape(-1)
    route_hits = (flat_routes[:, None] == jnp.arange(experts, dtype=jnp.int32)[None, :]).astype(
        jnp.int32
    )
    slot_rank = jnp.cumsum(route_hits, axis=0) - 1
    return jnp.sum(slot_rank * route_hits, axis=1).reshape(routes.shape)


def place_rows(rows_pair, routes, slot_index, experts, capacity):
    buffer = jnp.zeros((experts, capacity, rows_pair.shape[2]), rows_pair.dtype)
    return buffer.at[routes, slot_index].set(rows_pair)


def inner_rows(left_side, right_side):
    return lax.dot_general(
        left_side, right_side, (((0,), (0,)), ((), ())), preferred_element_type=jnp.float32
    )


def outer_cols(left_side, right_side):
    return lax.dot_general(
        left_side, right_side, (((1,), (1,)), ((), ())), preferred_element_type=jnp.float32
    )


def block_context(rel_bucket, segment, row_start, row_count, buckets):
    token_count = segment.shape[0]
    query_index = row_start + jnp.arange(row_count, dtype=jnp.int32)
    key_index = jnp.arange(token_count, dtype=jnp.int32)
    offset = jnp.clip(query_index[:, None] - key_index[None, :], 0, rel_bucket.shape[0] - 1)
    bucket_ids = jnp.arange(buckets, dtype=jnp.int32)
    bucket_start = jnp.sum((rel_bucket[None, :] < bucket_ids[:, None]).astype(jnp.int32), axis=1)
    bucket_end = jnp.sum((rel_bucket[None, :] <= bucket_ids[:, None]).astype(jnp.int32), axis=1)
    bucket_indicator = (
        (offset[None] >= bucket_start[:, None, None]) & (offset[None] < bucket_end[:, None, None])
    ).astype(jnp.bfloat16)
    allowed = (segment[:, None] == segment[None, :]) & (query_index[:, None] >= key_index[None, :])
    return (bucket_indicator, allowed)


def block_scores(
    query_block, key_heads, bucket_indicator, position_bias_table, allowed, score_scale
):
    raw_scores = (
        jnp.einsum("qhd,khd->hqk", query_block, key_heads, preferred_element_type=jnp.float32)
        * score_scale
    )
    raw_scores = raw_scores + jnp.einsum(
        "zd,dpv->zpv", position_bias_table, bucket_indicator, preferred_element_type=jnp.float32
    )
    return jnp.where(allowed[None], raw_scores, masked_value)


def norm_back(values, scale_inv, gain, grad_out):
    weighted = grad_out * gain
    grad_in = scale_inv * weighted - values * scale_inv**3 * jnp.mean(
        values * weighted, axis=-1, keepdims=True
    )
    grad_gain = jnp.sum(grad_out * values * scale_inv, axis=0)
    return (grad_in, grad_gain)


def gelu_tanh(values):
    return jax.nn.gelu(values, approximate=True)


def body(
    tokens,
    lengths,
    routes,
    rel_bucket,
    norm1,
    w_query,
    w_key,
    w_value,
    output_weight,
    position_bias_table,
    norm2,
    router,
    expert_in,
    expert_out,
    cotangent,
):
    token_count, model_width = tokens.shape
    local_heads, buckets = position_bias_table.shape
    head_size = w_query.shape[1] // local_heads
    experts = router.shape[1]
    top_count = routes.shape[1]
    capacity = 2 * top_count * token_count // experts
    row_count = min(512, token_count)
    score_scale = head_size ** (-0.5)
    gain_one = norm1.astype(jnp.float32)
    gain_two = norm2.astype(jnp.float32)
    inputs = tokens.astype(jnp.float32)
    segment = segment_ids(lengths[0], token_count)
    scale_one = lax.rsqrt(jnp.mean(inputs * inputs, axis=-1, keepdims=True) + epsilon)
    first_normed = (inputs * scale_one * gain_one).astype(jnp.bfloat16)
    query_proj = jnp.dot(first_normed, w_query, preferred_element_type=jnp.float32).astype(
        jnp.bfloat16
    )
    key_proj = jnp.dot(first_normed, w_key, preferred_element_type=jnp.float32).astype(jnp.bfloat16)
    value_proj = jnp.dot(first_normed, w_value, preferred_element_type=jnp.float32).astype(
        jnp.bfloat16
    )
    query_heads = query_proj.reshape(token_count, local_heads, head_size)
    key_heads = key_proj.reshape(token_count, local_heads, head_size)
    value_heads = value_proj.reshape(token_count, local_heads, head_size)
    block_index = 0
    row_start = block_index * row_count
    bucket_indicator, allowed = block_context(rel_bucket, segment, row_start, row_count, buckets)
    scores = block_scores(
        query_heads, key_heads, bucket_indicator, position_bias_table, allowed, score_scale
    )
    row_peak = jnp.max(scores, axis=2, keepdims=True)
    lifted = jnp.exp(scores - row_peak)
    row_total = jnp.sum(lifted, axis=2, keepdims=True)
    weights = (lifted / row_total).astype(jnp.bfloat16)
    attended_blocks = jnp.einsum(
        "hqk,khd->qhd", weights, value_heads, preferred_element_type=jnp.float32
    )
    log_sums = [row_peak + jnp.log(row_total)]
    attended = attended_blocks.reshape(token_count, local_heads * head_size).astype(jnp.bfloat16)
    branch = lax.psum(
        jnp.dot(attended, output_weight, preferred_element_type=jnp.float32), "tensor"
    )
    hidden_state = inputs + branch
    scale_two = lax.rsqrt(jnp.mean(hidden_state * hidden_state, axis=-1, keepdims=True) + epsilon)
    second_normed = (hidden_state * scale_two * gain_two).astype(jnp.bfloat16)
    logits = jnp.dot(second_normed, router, preferred_element_type=jnp.float32)
    chosen = jnp.take_along_axis(logits, routes, axis=1)
    gate_weights = jax.nn.softmax(chosen, axis=1)
    slot_index = route_slots(routes, experts)
    outgoing = place_rows(
        jnp.broadcast_to(second_normed[:, None, :], (token_count, top_count, model_width)),
        routes,
        slot_index,
        experts,
        capacity,
    )
    arrived = lax.all_to_all(outgoing, "dp", split_axis=0, concat_axis=1, tiled=True)
    pre_gelu = jnp.einsum("erd,edf->erf", arrived, expert_in, preferred_element_type=jnp.float32)
    activated = gelu_tanh(pre_gelu).astype(jnp.bfloat16)
    produced = jnp.einsum("erf,efd->erd", activated, expert_out, preferred_element_type=jnp.float32)
    returned = lax.all_to_all(
        produced.astype(jnp.bfloat16), "dp", split_axis=1, concat_axis=0, tiled=True
    ).astype(produced.dtype)
    expert_rows = lax.psum(returned[routes, slot_index].astype(jnp.bfloat16), "tensor").astype(
        jnp.float32
    )
    result = hidden_state + jnp.sum(gate_weights[:, :, None] * expert_rows, axis=1)
    layer_out = result.astype(jnp.bfloat16)
    grad_out = cotangent.astype(jnp.float32)
    grad_gate = jnp.sum(expert_rows * grad_out[:, None, :], axis=2)
    grad_chosen = gate_weights * (
        grad_gate - jnp.sum(gate_weights * grad_gate, axis=1, keepdims=True)
    )
    expert_ids = jnp.arange(experts, dtype=jnp.int32)
    grad_logits = jnp.sum(
        (routes[:, :, None] == expert_ids).astype(jnp.float32) * grad_chosen[:, :, None], axis=1
    )
    normed_wide = second_normed.astype(jnp.float32)
    router_wide = router.astype(jnp.float32)
    grad_router = jnp.dot(normed_wide.T, grad_logits, precision=lax.Precision.HIGHEST)
    grad_from_router = jnp.dot(grad_logits, router_wide.T, precision=lax.Precision.HIGHEST)
    grad_rows = (gate_weights[:, :, None] * grad_out[:, None, :]).astype(jnp.bfloat16)
    grad_arrived = lax.all_to_all(
        place_rows(grad_rows, routes, slot_index, experts, capacity),
        "dp",
        split_axis=0,
        concat_axis=1,
        tiled=True,
    )
    grad_act = jnp.einsum(
        "erd,efd->erf", grad_arrived, expert_out, preferred_element_type=jnp.float32
    )
    grad_pre = jax.vjp(gelu_tanh, pre_gelu)[1](grad_act)[0].astype(jnp.bfloat16)
    grad_expert_out = jnp.einsum(
        "erf,erd->efd", activated, grad_arrived, preferred_element_type=jnp.float32
    )
    grad_expert_in = jnp.einsum(
        "erd,erf->edf", arrived, grad_pre, preferred_element_type=jnp.float32
    )
    grad_inputs = jnp.einsum(
        "erf,edf->erd", grad_pre, expert_in, preferred_element_type=jnp.float32
    )
    grad_returned = lax.all_to_all(
        grad_inputs.astype(jnp.bfloat16), "dp", split_axis=1, concat_axis=0, tiled=True
    ).astype(grad_inputs.dtype)
    grad_expert_tokens = jnp.sum(grad_returned[routes, slot_index], axis=1)
    grad_normed_two = (
        lax.psum(grad_expert_tokens.astype(jnp.bfloat16), "tensor").astype(jnp.float32)
        + grad_from_router
    )
    grad_hidden, grad_norm2 = norm_back(hidden_state, scale_two, gain_two, grad_normed_two)
    grad_hidden = grad_out + grad_hidden
    grad_branch = grad_hidden.astype(jnp.bfloat16)
    grad_w_output = inner_rows(attended, grad_branch)
    grad_attended = outer_cols(grad_branch, output_weight).astype(jnp.bfloat16)
    grad_attended_heads = grad_attended.reshape(token_count, local_heads, head_size)
    block_index = 0
    row_start = block_index * row_count
    bucket_indicator, allowed = block_context(rel_bucket, segment, row_start, row_count, buckets)
    scores = block_scores(
        query_heads, key_heads, bucket_indicator, position_bias_table, allowed, score_scale
    )
    probs = jnp.exp(scores - log_sums[block_index])
    probs_low = probs.astype(jnp.bfloat16)
    grad_value_sum = jnp.einsum(
        "hqk,qhd->khd", probs_low, grad_attended_heads, preferred_element_type=jnp.float32
    )
    grad_probs = jnp.einsum(
        "qhd,khd->hqk", grad_attended_heads, value_heads, preferred_element_type=jnp.float32
    )
    row_delta = jnp.sum(probs * grad_probs, axis=2, keepdims=True)
    gradient_attention_scores = (probs * (grad_probs - row_delta)).astype(jnp.bfloat16)
    grad_query_blocks = (
        jnp.einsum(
            "hqk,khd->qhd", gradient_attention_scores, key_heads, preferred_element_type=jnp.float32
        )
        * score_scale
    )
    grad_key_sum = (
        jnp.einsum(
            "hqk,qhd->khd",
            gradient_attention_scores,
            query_heads,
            preferred_element_type=jnp.float32,
        )
        * score_scale
    )
    gradient_bias_table = jnp.einsum(
        "ruo,vuo->rv",
        gradient_attention_scores,
        bucket_indicator,
        preferred_element_type=jnp.float32,
    )
    grad_query_low = grad_query_blocks.reshape(token_count, local_heads * head_size).astype(
        jnp.bfloat16
    )
    grad_key_low = grad_key_sum.reshape(token_count, local_heads * head_size).astype(jnp.bfloat16)
    grad_value_low = grad_value_sum.reshape(token_count, local_heads * head_size).astype(
        jnp.bfloat16
    )
    grad_w_query = inner_rows(first_normed, grad_query_low)
    grad_w_key = inner_rows(first_normed, grad_key_low)
    grad_w_value = inner_rows(first_normed, grad_value_low)
    gradient_normalized_piece = (
        outer_cols(grad_query_low, w_query)
        + outer_cols(grad_key_low, w_key)
        + outer_cols(grad_value_low, w_value)
    )
    grad_normed_one = lax.psum(gradient_normalized_piece.astype(jnp.bfloat16), "tensor").astype(
        jnp.float32
    )
    grad_input, grad_norm1 = norm_back(inputs, scale_one, gain_one, grad_normed_one)
    grad_tokens = grad_hidden + grad_input
    summed = lax.psum(
        (
            grad_w_query,
            grad_w_key,
            grad_w_value,
            grad_w_output,
            gradient_bias_table,
            grad_norm1,
            grad_norm2,
            grad_router,
        ),
        "dp",
    )
    return (
        layer_out,
        grad_tokens,
        summed[5],
        summed[0],
        summed[1],
        summed[2],
        summed[3],
        summed[4],
        summed[6],
        summed[7],
        grad_expert_in,
        grad_expert_out,
    )


def solution(mesh):
    in_specs = (
        P("dp", None),
        P("dp", None),
        P("dp", None),
        P(),
        P(),
        P(None, "tensor"),
        P(None, "tensor"),
        P(None, "tensor"),
        P("tensor", None),
        P("tensor", None),
        P(),
        P(),
        P("dp", None, "tensor"),
        P("dp", "tensor", None),
        P("dp", None),
    )
    out_specs = (
        P("dp", None),
        P("dp", None),
        P(),
        P(None, "tensor"),
        P(None, "tensor"),
        P(None, "tensor"),
        P("tensor", None),
        P("tensor", None),
        P(),
        P(),
        P("dp", None, "tensor"),
        P("dp", "tensor", None),
    )
    return jax.shard_map(body, mesh=mesh, in_specs=in_specs, out_specs=out_specs, check_vma=False)
```

```python
import functools

import jax
import jax.numpy as jnp
from jax import lax
from jax.experimental import pallas as pl
from jax.experimental.pallas import tpu as pltpu
from jax.sharding import PartitionSpec as P

epsilon = 1e-06
masked_value = -1e30
bf16 = jnp.bfloat16
f32 = jnp.float32
VMEM = pl.BlockSpec(memory_space=pltpu.VMEM)
SMEM = pl.BlockSpec(memory_space=pltpu.SMEM)
vmem_bytes = 56 * 1024 * 1024
expert_vmem_bytes = vmem_bytes
gelu_root = 0.7978845608028654
gelu_cubic = 0.044715


def mm(left, right, left_dim=1, right_dim=0, precision=None):
    return lax.dot_general(
        left,
        right,
        (((left_dim,), (right_dim,)), ((), ())),
        preferred_element_type=f32,
        precision=precision,
    )


def gain_row(ref):
    return ref[...].astype(f32).reshape(1, ref.shape[0])


def iota(shape, dim):
    return lax.broadcasted_iota(jnp.int32, shape, dim)


def call(kernel, out_shape, operands, specs, flops, nbytes, **options):
    return pl.pallas_call(
        kernel,
        out_shape=out_shape,
        in_specs=specs,
        compiler_params=pltpu.CompilerParams(vmem_limit_bytes=vmem_bytes),
        cost_estimate=pl.CostEstimate(flops=flops, bytes_accessed=nbytes, transcendentals=0),
        **options,
    )(*operands)


def half(ref_or_width, which, width):
    return pl.ds(pl.multiple_of(which * width, 128), width)


def route_kernel(place_ref, routes_ref, cotangent_ref, placing_ref, payload_ref, *, experts, capacity):
    tokens = routes_ref.shape[1]
    groups, padded_rows, width = payload_ref.shape
    rows = experts * capacity // groups
    sent = padded_rows - 16
    core = place_ref[0]
    ids = iota((experts, tokens), 0)
    hit = ((routes_ref[0:1, :] == ids) | (routes_ref[1:2, :] == ids)).astype(f32)
    earlier = (iota((tokens, tokens), 0) < iota((tokens, tokens), 1)).astype(bf16)
    rank = mm(hit.astype(bf16), earlier)
    slot = jnp.where(hit > 0.5, rank, -1.0)
    id_sum = jnp.sum(hit * ids.astype(f32), axis=0, keepdims=True)
    id_sum = jnp.broadcast_to(id_sum, (16, tokens)).astype(bf16)
    slot_iota = iota((capacity, tokens), 0).astype(f32)
    for e in range(experts):
        placing_ref[e * capacity : (e + 1) * capacity, :] = (slot[e : e + 1, :] == slot_iota).astype(bf16)
    grad_half = cotangent_ref[:, half(None, core, width)]
    start = 0 if sent == rows else place_ref[2] * sent
    for d in range(groups):
        placed = placing_ref[pl.ds(pl.multiple_of(d * rows + start, 16), sent), :]
        payload_ref[d, 0:sent, :] = mm(placed, grad_half).astype(bf16)
        slot_ids = mm(id_sum, placed, 1, 1).astype(bf16)
        payload_ref[d, sent : sent + 16, :] = jnp.concatenate(
            [slot_ids, jnp.zeros((16, width - sent), bf16)], axis=1
        )


def bucket_rows(rel_bucket_ref, span, buckets):
    offsets = rel_bucket_ref.shape[1]
    backwards = (iota((offsets, span), 0) == span - 1 - iota((offsets, span), 1)).astype(bf16)
    table = jnp.broadcast_to(rel_bucket_ref[...].astype(f32), (16, offsets)).astype(bf16)
    reversed_bucket = mm(table, backwards)[0:1, :]
    return reversed_bucket == iota((buckets, span), 0).astype(f32)


def attention_kernel(
    lengths_ref,
    tokens_ref,
    rel_bucket_ref,
    norm1_ref,
    wq_ref,
    wk_ref,
    wv_ref,
    table_ref,
    attended_ref,
    q_ref,
    k_ref,
    v_ref,
    probs_ref,
):
    span = tokens_ref.shape[0]
    heads, buckets = table_ref.shape
    size = wq_ref.shape[0] // heads
    x = tokens_ref[...].astype(f32)
    r1 = lax.rsqrt(jnp.mean(x * x, axis=1, keepdims=True) + epsilon)
    normed = (x * r1 * gain_row(norm1_ref)).astype(bf16)
    q = mm(normed, wq_ref[...], 1, 1).astype(bf16)
    k = mm(normed, wk_ref[...], 1, 1).astype(bf16)
    v = mm(normed, wv_ref[...], 1, 1).astype(bf16)
    q_ref[...] = q
    k_ref[...] = k
    v_ref[...] = v
    query_index = iota((span, 1), 0)
    key_index = iota((1, span), 1)
    query_segment = jnp.zeros((span, 1), jnp.int32)
    key_segment = jnp.zeros((1, span), jnp.int32)
    end = jnp.int32(0)
    for j in range(lengths_ref.shape[1]):
        end = end + lengths_ref[0, j]
        query_segment = query_segment + (query_index >= end).astype(jnp.int32)
        key_segment = key_segment + (key_index >= end).astype(jnp.int32)
    allowed = (query_segment == key_segment) & (query_index >= key_index)
    indicator = bucket_rows(rel_bucket_ref, span, buckets).astype(bf16)
    bias_rows = mm(table_ref[...], indicator)
    outs = []
    for h in range(heads):
        cut = slice(h * size, (h + 1) * size)
        bias = jnp.broadcast_to(bias_rows[h : h + 1, :], (span, span))
        bias = pltpu.roll(bias, 1, 1, stride=1, stride_axis=0)
        scores = mm(q[:, cut], k[:, cut], 1, 1) * (size**-0.5) + bias
        scores = jnp.where(allowed, scores, masked_value)
        lifted = jnp.exp(scores - jnp.max(scores, axis=1, keepdims=True))
        probs = lifted / jnp.sum(lifted, axis=1, keepdims=True)
        probs_ref[h] = probs
        outs.append(mm(probs.astype(bf16), v[:, cut]))
    attended_ref[...] = jnp.concatenate(outs, axis=1).astype(bf16)


def hidden_kernel(
    core_ref,
    tokens_ref,
    a0_ref,
    a1_ref,
    a2_ref,
    a3_ref,
    w0_ref,
    w1_ref,
    w2_ref,
    w3_ref,
    norm2_ref,
    placing_ref,
    hidden_ref,
    payload_ref,
    normed_ref,
    heads_ref,
    weights_ref,
):
    groups, rows, width = payload_ref.shape
    core, far = core_ref[0], core_ref[2]
    parts = ((a0_ref, w0_ref), (a1_ref, w1_ref), (a2_ref, w2_ref), (a3_ref, w3_ref))
    for bits, (a, w) in enumerate(parts):
        index = (far ^ (bits // 2)) * 2 + (core ^ (bits % 2))
        heads_ref[index] = a[...]
        weights_ref[index] = w[...]
    hidden = tokens_ref[...].astype(f32)
    for index in range(4):
        hidden = hidden + mm(heads_ref[index], weights_ref[index])
    hidden_ref[...] = hidden
    r2 = lax.rsqrt(jnp.mean(hidden * hidden, axis=1, keepdims=True) + epsilon)
    normed_ref[...] = (hidden * r2 * gain_row(norm2_ref)).astype(bf16)
    normed_half = normed_ref[:, half(None, core_ref[0], width)]
    for d in range(groups):
        payload_ref[d] = mm(placing_ref[d * rows : (d + 1) * rows, :], normed_half).astype(bf16)


def merge_rows(ref):
    a, b, c = ref.shape
    return ref[...].reshape(a * b, c)


def cotangent_kernel(place_ref, *refs, halves, share):
    ids_refs, own_refs, oth_refs = refs[:halves], refs[halves : 2 * halves], refs[2 * halves : 3 * halves]
    w_out_ref, back_ref, rows_ref, other_ref = refs[3 * halves :]
    e = pl.program_id(0)
    blocks, capacity, width = own_refs[0].shape
    rows = blocks * capacity
    experts = other_ref.shape[2]
    core = place_ref[0]
    own = half(None, core, width)
    oth = half(None, 1 - core, width)
    ids = [r[:, 0:1, :].astype(f32) for r in ids_refs]
    g_own, g_oth = [merge_rows(r) for r in own_refs], [merge_rows(r) for r in oth_refs]
    if halves == 2:
        mine = e // share == place_ref[2]
        ids, g_own, g_oth = (jnp.where(mine, pair[0], pair[1]) for pair in (ids, g_own, g_oth))
    else:
        ids, g_own, g_oth = ids[0], g_own[0], g_oth[0]
    ids = jnp.broadcast_to(ids, (blocks, capacity, width)).reshape(rows, width)
    lane = iota((rows, width), 1)
    slot = lax.rem(iota((rows, width), 0), capacity)
    id_sum = jnp.sum(
        jnp.where(lane == lax.rem(e, share) * capacity + slot, ids, 0.0), axis=1, keepdims=True
    )
    other = id_sum.astype(jnp.int32) - (place_ref[1] + e)
    other_ref[0] = (iota((rows, experts), 1) == other).astype(bf16)
    rows_ref[0, :, own] = g_own
    rows_ref[0, :, oth] = g_oth
    back = mm(g_own, w_out_ref[0, :, own], 1, 1) + mm(g_oth, w_out_ref[0, :, oth], 1, 1)
    back_ref[0] = back.astype(bf16)


def expert_grad_kernel(
    place_ref,
    n_own_ref,
    n_oth_ref,
    back_ref,
    other_ref,
    router_ref,
    w_in_ref,
    w_out_ref,
    keep_ref,
    send_ref,
    act_ref,
    pre_ref,
    y_keep_ref,
    y_send_ref,
    grad_router_ref,
):
    blocks, capacity, width = n_own_ref.shape
    rows = blocks * capacity
    experts = router_ref.shape[0]
    units = pre_ref.shape[2]
    core = place_ref[0]
    own = half(None, core, width)
    oth = half(None, 1 - core, width)
    n_own, n_oth = merge_rows(n_own_ref), merge_rows(n_oth_ref)
    is_own = iota((rows, experts), 1) == place_ref[1] + pl.program_id(0)
    is_other = other_ref[0].astype(f32)
    logits = mm(n_own, router_ref[:, own], 1, 1) + mm(n_oth, router_ref[:, oth], 1, 1)
    logit_own = jnp.sum(jnp.where(is_own, logits, 0.0), axis=1, keepdims=True)
    logit_other = jnp.sum(is_other * logits, axis=1, keepdims=True)
    peak = jnp.maximum(logit_own, logit_other)
    up_own, up_other = jnp.exp(logit_own - peak), jnp.exp(logit_other - peak)
    gate = up_own / (up_own + up_other)
    grad_gate = jnp.zeros((rows, 1), f32)
    step = 256 if units % 256 == 0 else units
    for start in range(0, units, step):
        cut = slice(start, start + step)
        pre = mm(n_own, w_in_ref[0, own, cut]) + mm(n_oth, w_in_ref[0, oth, cut])
        square = pre * pre
        bend = jnp.tanh(pre * (gelu_root + gelu_root * gelu_cubic * square))
        rise = 0.5 + 0.5 * bend
        act = pre * rise
        slope = rise + act * (1.0 - bend) * (gelu_root + 3.0 * gelu_root * gelu_cubic * square)
        back = gate * back_ref[0, :, cut].astype(f32)
        grad_gate = grad_gate + jnp.sum(act * back, axis=1, keepdims=True)
        act_ref[0, :, cut] = (gate * act).astype(bf16)
        pre_ref[0, :, cut] = (back * slope).astype(bf16)
    grad_logit = grad_gate * (up_other / (up_own + up_other))
    coefficient = (jnp.where(is_own, grad_logit, 0.0) - is_other * grad_logit).astype(bf16)

    @pl.when((pl.program_id(0) == 0) & (pl.program_id(1) == 0))
    def _():
        grad_router_ref[...] = jnp.zeros_like(grad_router_ref)

    grad_router_ref[:, own] += mm(coefficient, n_own, 0, 0)
    grad_router_ref[:, oth] += mm(coefficient, n_oth, 0, 0)
    y_send_ref[...] = mm(act_ref[0], w_out_ref[0, :, oth]).astype(bf16).reshape(y_send_ref.shape)
    y_keep_ref[...] = mm(act_ref[0], w_out_ref[0, :, own]).astype(bf16).reshape(y_keep_ref.shape)

    def grad_in(cut):
        rows_back = mm(pre_ref[0], w_in_ref[0, cut, :], 1, 1)
        rows_back = rows_back + mm(coefficient, router_ref[:, cut])
        return rows_back.astype(bf16).reshape(blocks, capacity, width)

    send_ref[...] = grad_in(oth)
    keep_ref[...] = grad_in(own)


def expert_weight_kernel(
    place_ref, n_own_ref, n_oth_ref, g_ref, act_ref, pre_ref, grad_in_ref, grad_out_ref
):
    width = n_own_ref.shape[2]
    core = place_ref[0]
    act, grad_pre = act_ref[0], pre_ref[0]
    parts = (
        (half(None, core, width), merge_rows(n_own_ref)),
        (half(None, 1 - core, width), merge_rows(n_oth_ref)),
    )

    @pl.when(pl.program_id(1) == 0)
    def _():
        grad_out_ref[0] = mm(act, g_ref[0], 0, 0)
        for cut, n in parts:
            grad_in_ref[0, cut, :] = mm(n, grad_pre, 0, 0)

    @pl.when(pl.program_id(1) > 0)
    def _():
        grad_out_ref[0] += mm(act, g_ref[0], 0, 0)
        for cut, n in parts:
            grad_in_ref[0, cut, :] += mm(n, grad_pre, 0, 0)


def combine_kernel(place_ref, placing_ref, rows_ref, out_ref):
    groups, rows, width = rows_ref.shape
    placing = placing_ref[...].reshape(groups * rows, placing_ref.shape[3])
    out_ref[...] = mm(placing, rows_ref[...].reshape(groups * rows, width), 0, 0).astype(bf16)


def attention_back_kernel(
    core_ref,
    z0_ref,
    z1_ref,
    z2_ref,
    z3_ref,
    hidden_ref,
    cotangent_ref,
    tokens_ref,
    norm1_ref,
    norm2_ref,
    wo_ref,
    attended_ref,
    q_ref,
    k_ref,
    v_ref,
    probs_ref,
    rel_bucket_ref,
    grad_router_ref,
    grad_hidden_ref,
    weights_ref,
    low_ref,
    gn_ref,
):
    span, model = hidden_ref.shape
    heads = probs_ref.shape[0]
    size = q_ref.shape[1] // heads
    inner = q_ref.shape[1]
    width = z0_ref.shape[1]
    core = core_ref[0]
    own = half(None, core, width)
    oth = half(None, 1 - core, width)
    gn_ref[:, own] = z0_ref[...].astype(f32) + z2_ref[...].astype(f32)
    gn_ref[:, oth] = z1_ref[...].astype(f32) + z3_ref[...].astype(f32)
    grad_normed = gn_ref[...]
    hidden = hidden_ref[...]
    r2 = lax.rsqrt(jnp.mean(hidden * hidden, axis=1, keepdims=True) + epsilon)
    weighted = grad_normed * gain_row(norm2_ref)
    inner_mean = jnp.mean(hidden * weighted, axis=1, keepdims=True)
    grad_hidden = cotangent_ref[...].astype(f32) + (r2 * weighted - hidden * (r2 * r2 * r2) * inner_mean)
    grad_hidden_ref[...] = grad_hidden
    grad_norm2 = jnp.sum(grad_normed * hidden * r2, axis=0, keepdims=True)
    branch = grad_hidden.astype(bf16)
    weights_ref[3 * inner : 4 * inner, :] = mm(attended_ref[...], branch, 0, 0).astype(bf16)
    grad_attended = mm(branch, wo_ref[...], 1, 1).astype(bf16)
    indicator = bucket_rows(rel_bucket_ref, span, 128).astype(f32)
    flip = (iota((span, span), 0) + iota((span, span), 1) == span - 1).astype(bf16)
    q, k, v = q_ref[...], k_ref[...], v_ref[...]
    dq, dk, dv, diagonals = [], [], [], []
    for h in range(heads):
        cut = slice(h * size, (h + 1) * size)
        probs = probs_ref[h]
        ga = grad_attended[:, cut]
        dv.append(mm(probs.astype(bf16), ga, 0, 0))
        grad_probs = mm(ga, v[:, cut], 1, 1)
        delta = jnp.sum(probs * grad_probs, axis=1, keepdims=True)
        ds = (probs * (grad_probs - delta)).astype(bf16)
        dq.append(mm(ds, k[:, cut]) * (size**-0.5))
        dk.append(mm(ds, q[:, cut], 0, 0) * (size**-0.5))
        rolled = pltpu.roll(mm(flip, ds), 0, 1, stride=1, stride_axis=0)
        diagonals.append(jnp.sum(rolled, axis=0, keepdims=True))
    diagonals = jnp.concatenate(diagonals + [jnp.zeros((8 - heads, span), f32)], axis=0)
    bias = mm(diagonals, indicator, 1, 1, lax.Precision.HIGHEST)
    small = jnp.concatenate(
        [
            jnp.concatenate([bias, jnp.zeros((8, model - 128), f32)], axis=1),
            jnp.broadcast_to(grad_norm2, (8, model)),
        ],
        axis=0,
    )
    x = tokens_ref[...].astype(f32)
    r1 = lax.rsqrt(jnp.mean(x * x, axis=1, keepdims=True) + epsilon)
    normed = (x * r1 * gain_row(norm1_ref)).astype(bf16)
    for j, parts in enumerate((dq, dk, dv)):
        low = jnp.concatenate(parts, axis=1).astype(bf16)
        low_ref[j] = low
        weights_ref[j * inner : (j + 1) * inner, :] = mm(low, normed, 0, 0).astype(bf16)
    end = 4 * inner
    experts = grad_router_ref.shape[0]
    weights_ref[end : end + experts, :] = grad_router_ref[...].astype(bf16)
    end = end + experts
    weights_ref[end : end + 16, :] = small.astype(bf16)
    weights_ref[end + 16 :, :] = jnp.zeros((weights_ref.shape[0] - end - 16, model), bf16)


def input_back_kernel(core_ref, low_ref, wq_ref, wk_ref, wv_ref, keep_ref, send_ref, piece_ref):
    width = keep_ref.shape[1]
    core = core_ref[0]
    piece_ref[...] = (
        mm(low_ref[0], wq_ref[...])
        + mm(low_ref[1], wk_ref[...])
        + mm(low_ref[2], wv_ref[...])
    )
    keep_ref[...] = piece_ref[:, half(None, core, width)]
    send_ref[...] = piece_ref[:, half(None, 1 - core, width)].astype(bf16)


def finish_kernel(
    core_ref,
    u0_ref,
    u1_ref,
    u2_ref,
    u3_ref,
    grad_hidden_ref,
    tokens_ref,
    norm1_ref,
    out_ref,
    norm_row_ref,
    gn_ref,
):
    width = u0_ref.shape[1]
    core = core_ref[0]
    gn_ref[:, half(None, core, width)] = u0_ref[...].astype(f32) + u2_ref[...].astype(f32)
    gn_ref[:, half(None, 1 - core, width)] = u1_ref[...].astype(f32) + u3_ref[...].astype(f32)
    x = tokens_ref[...].astype(f32)
    r1 = lax.rsqrt(jnp.mean(x * x, axis=1, keepdims=True) + epsilon)
    grad_normed = gn_ref[...]
    weighted = grad_normed * gain_row(norm1_ref)
    inner_mean = jnp.mean(x * weighted, axis=1, keepdims=True)
    out_ref[...] = grad_hidden_ref[...] + (r1 * weighted - x * (r1 * r1 * r1) * inner_mean)
    row = jnp.sum(grad_normed * x * r1, axis=0, keepdims=True)
    norm_row_ref[...] = jnp.broadcast_to(row, norm_row_ref.shape).astype(bf16)


def chunk_kernel(rows_ref, norm_row_ref, out_ref):
    groups, chunk, _ = rows_ref.shape
    total = rows_ref[0].astype(f32)
    for d in range(1, groups):
        total = total + rows_ref[d].astype(f32)
    total = total.astype(bf16)
    for d in range(groups):
        out_ref[d, 0:chunk, :] = total
        out_ref[d, chunk : chunk + 16, :] = norm_row_ref[...]


def unpack_kernel(
    rows_ref, norm1_ref, wq_ref, wk_ref, wv_ref, wo_ref, bias_ref, norm2_ref, router_ref, all_ref
):
    groups, padded, _ = rows_ref.shape
    chunk = padded - 16
    inner = wo_ref.shape[0]
    experts = router_ref.shape[0]
    heads, buckets = bias_ref.shape
    norm1 = rows_ref[0, chunk : chunk + 1, :].astype(f32)
    for d in range(groups):
        all_ref[d * chunk : (d + 1) * chunk, :] = rows_ref[d, 0:chunk, :]
        if d:
            norm1 = norm1 + rows_ref[d, chunk : chunk + 1, :].astype(f32)
    norm1_ref[...] = norm1.reshape(norm1_ref.shape)
    for j, out in enumerate((wq_ref, wk_ref, wv_ref)):
        out[...] = all_ref[j * inner : (j + 1) * inner, :].astype(f32)
    wo_ref[...] = all_ref[3 * inner : 4 * inner, :].astype(f32)
    end = 4 * inner
    router_ref[...] = all_ref[end : end + experts, :].astype(f32)
    small = all_ref[end + experts : end + experts + 16, :].astype(f32)
    bias_ref[...] = small[0:heads, 0:buckets]
    norm2_ref[...] = small[8:9, :].reshape(norm2_ref.shape)


def layer_out_kernel(core_ref, y0_ref, y1_ref, y2_ref, y3_ref, hidden_ref, out_ref):
    width = y0_ref.shape[1]
    core = core_ref[0]
    own = half(None, core, width)
    oth = half(None, 1 - core, width)
    out_ref[:, own] = (
        hidden_ref[:, own] + (y0_ref[...].astype(f32) + y2_ref[...].astype(f32))
    ).astype(bf16)
    out_ref[:, oth] = (
        hidden_ref[:, oth] + (y1_ref[...].astype(f32) + y3_ref[...].astype(f32))
    ).astype(bf16)


def struct(shape, dtype):
    return jax.ShapeDtypeStruct(shape, dtype)


def body(
    groups,
    lanes,
    tokens,
    lengths,
    routes,
    rel_bucket,
    norm1,
    w_query,
    w_key,
    w_value,
    output_weight,
    position_bias_table,
    norm2,
    router,
    expert_in,
    expert_out,
    cotangent,
):
    span, model = tokens.shape
    heads, buckets = position_bias_table.shape
    inner = w_query.shape[1]
    experts = router.shape[1]
    local_experts, _, hidden_units = expert_in.shape
    capacity = 2 * routes.shape[1] * span // experts
    rows = local_experts * capacity
    width = model // 2
    rel_bucket = rel_bucket.reshape(1, -1)
    member = lax.axis_index("tensor")
    group = lax.axis_index("dp")
    place = jnp.stack([lax.rem(member, 2), group * local_experts, member // 2]).astype(jnp.int32)
    halves = 2 if local_experts % 2 == 0 else 1
    share = local_experts // halves
    sent = rows // halves

    def swap(value, bits):
        return lax.ppermute(value, "tensor", [(i, i ^ bits) for i in range(lanes)])

    def spread(value):
        far = swap(value, 2)
        return value, swap(value, 1), far, swap(far, 1)

    def exchange(value):
        return lax.all_to_all(value, "dp", split_axis=0, concat_axis=0, tiled=True)

    def add_low(left, right):
        return (left.astype(f32) + right.astype(f32)).astype(bf16)

    placing, grad_payload = call(
        functools.partial(route_kernel, experts=experts, capacity=capacity),
        (
            struct((experts * capacity, span), bf16),
            struct((groups, sent + 16, width), bf16),
        ),
        (place, routes.T, cotangent),
        [SMEM, VMEM, VMEM],
        3 * 10**9,
        6 * 10**6,
    )
    g_rows = [exchange(grad_payload)]
    if halves == 2:
        g_rows.append(swap(g_rows[0], 2))
    g_others = [swap(value, 1) for value in g_rows]
    output_weights = spread(output_weight)
    attended, q, k, v, probs = call(
        attention_kernel,
        (
            struct((span, inner), bf16),
            struct((span, inner), bf16),
            struct((span, inner), bf16),
            struct((span, inner), bf16),
            struct((heads, span, span), f32),
        ),
        (lengths, tokens, rel_bucket, norm1, w_query.T, w_key.T, w_value.T, position_bias_table),
        [SMEM] + [VMEM] * 7,
        6 * 10**9,
        8 * 10**6,
    )
    attended_all = spread(attended)
    hidden, payload = call(
        hidden_kernel,
        (struct((span, model), f32), struct((groups, rows, width), bf16)),
        (place, tokens) + attended_all + output_weights + (norm2, placing),
        [SMEM] + [VMEM] * 11,
        2 * 10**9,
        8 * 10**6,
        scratch_shapes=[
            pltpu.VMEM((span, model), bf16),
            pltpu.VMEM((4, span, inner), bf16),
            pltpu.VMEM((4, inner, model), bf16),
        ],
    )
    n_own = exchange(payload)

    blocks = min(groups, 8)
    steps = groups // blocks
    block_rows = blocks * capacity
    row_spec = pl.BlockSpec((blocks, capacity, width), lambda e, j, p: (j, e, 0))

    def half_spec(which):
        def index(e, j, p):
            first = (p[2] ^ which) * share if halves == 2 else 0
            return (j, jnp.clip(e - first, 0, share - 1), 0)

        return pl.BlockSpec((blocks, capacity, width), index)

    ids_spec = pl.BlockSpec((blocks, 16, width), lambda e, j, p: (j, sent // 16, 0))

    def kept_spec(columns):
        return pl.BlockSpec((1, block_rows, columns), lambda e, j, p: (e, j, 0))

    in_spec = pl.BlockSpec((1, model, hidden_units), lambda e, j, p: (e, 0, 0))
    out_spec = pl.BlockSpec((1, hidden_units, model), lambda e, j, p: (e, 0, 0))
    router_spec = pl.BlockSpec((experts, model), lambda e, j, p: (0, 0))
    row_struct = struct((groups, rows, width), bf16)
    unit = 2 * groups * rows * model * hidden_units

    def kept_struct(columns):
        return struct((local_experts, groups * capacity, columns), bf16)

    def expert_call(kernel, out_shape, operands, in_specs, out_specs, flops, nbytes):
        return pl.pallas_call(
            kernel,
            out_shape=out_shape,
            grid_spec=pltpu.PrefetchScalarGridSpec(
                num_scalar_prefetch=1,
                grid=(local_experts, steps),
                in_specs=in_specs,
                out_specs=out_specs,
            ),
            compiler_params=pltpu.CompilerParams(vmem_limit_bytes=expert_vmem_bytes),
            cost_estimate=pl.CostEstimate(flops=flops, bytes_accessed=nbytes, transcendentals=0),
        )(place, *operands)

    which = range(halves)
    back, g_full, other = expert_call(
        functools.partial(cotangent_kernel, halves=halves, share=share),
        (kept_struct(hidden_units), kept_struct(model), kept_struct(experts)),
        (*g_rows, *g_rows, *g_others, expert_out),
        [ids_spec] * halves + [half_spec(w) for w in which] * 2 + [out_spec],
        (kept_spec(hidden_units), kept_spec(model), kept_spec(experts)),
        unit,
        20 * 10**6,
    )
    n_own, back, g_full, other = lax.optimization_barrier((n_own, back, g_full, other))
    n_oth = swap(n_own, 1)
    if halves == 2:
        y_struct = struct((2, groups, sent, width), bf16)
        y_spec = pl.BlockSpec(
            (1, blocks, capacity, width),
            lambda e, j, p: ((e // share) ^ p[2], j, lax.rem(e, share), 0),
        )
    else:
        y_struct, y_spec = row_struct, row_spec
    keep, send, act, grad_pre, y_keep, y_send, grad_router = expert_call(
        expert_grad_kernel,
        (
            row_struct,
            row_struct,
            kept_struct(hidden_units),
            kept_struct(hidden_units),
            y_struct,
            y_struct,
            struct((experts, model), f32),
        ),
        (n_own, n_oth, back, other, router.T, expert_in, expert_out),
        [row_spec, row_spec, kept_spec(hidden_units), kept_spec(experts)]
        + [router_spec, in_spec, out_spec],
        (row_spec, row_spec, kept_spec(hidden_units), kept_spec(hidden_units))
        + (y_spec, y_spec, router_spec),
        3 * unit,
        35 * 10**6,
    )
    back_rows = add_low(keep, swap(send, 1))
    back_rows, y_send = lax.optimization_barrier((back_rows, y_send))
    back_rows = exchange(back_rows)
    y_rows = add_low(y_keep, swap(y_send, 1))
    y_far = swap(y_rows[1], 2) if halves == 2 else None
    grad_router = grad_router + swap(grad_router, 1)
    grad_router = grad_router + swap(grad_router, 2)


    def combine(value):
        count = value.shape[1]
        parted = placing.reshape(groups, rows // count, count, span)
        return pl.pallas_call(
            combine_kernel,
            out_shape=struct((span, width), bf16),
            grid_spec=pltpu.PrefetchScalarGridSpec(
                num_scalar_prefetch=1,
                grid=(1,),
                in_specs=[
                    pl.BlockSpec(
                        (groups, 1, count, span),
                        lambda i, p: (0, p[2] if count < rows else 0, 0, 0),
                    ),
                    pl.BlockSpec((groups, count, width), lambda i, p: (0, 0, 0)),
                ],
                out_specs=pl.BlockSpec((span, width), lambda i, p: (0, 0)),
            ),
            compiler_params=pltpu.CompilerParams(vmem_limit_bytes=vmem_bytes),
            cost_estimate=pl.CostEstimate(flops=10**9, bytes_accessed=4 * 10**6, transcendentals=0),
        )(place, parted, value)

    back_rows, grad_router = lax.optimization_barrier((back_rows, grad_router))
    z = combine(back_rows)
    if halves == 2:
        z, y_far = lax.optimization_barrier((z, y_far))
        y_rows = add_low(y_rows[0], y_far)
    y_rows = exchange(y_rows)
    z = spread(z)
    chunk = -(-(4 * inner + experts + 16) // (16 * groups)) * 16
    grad_hidden, weights, low = call(
        attention_back_kernel,
        (
            struct((span, model), f32),
            struct((groups * chunk, model), bf16),
            struct((3, span, inner), bf16),
        ),
        (place,)
        + z
        + (hidden, cotangent, tokens, norm1, norm2, output_weight)
        + (attended, q, k, v, probs, rel_bucket, grad_router),
        [SMEM] + [VMEM] * 17,
        10 * 10**9,
        14 * 10**6,
        scratch_shapes=[pltpu.VMEM((span, model), f32)],
    )
    weights, y_rows = lax.optimization_barrier((weights, y_rows))
    weight_rows = exchange(weights.reshape(groups, chunk, model))
    piece_keep, piece_send = call(
        input_back_kernel,
        (struct((span, width), f32), struct((span, width), bf16)),
        (place, low, w_query.T, w_key.T, w_value.T),
        [SMEM] + [VMEM] * 4,
        10**9,
        4 * 10**6,
        scratch_shapes=[pltpu.VMEM((span, model), f32)],
    )
    piece = add_low(piece_keep, swap(piece_send, 1))
    grad_tokens, norm_row = call(
        finish_kernel,
        (struct((span, model), f32), struct((16, model), bf16)),
        (place,) + spread(piece) + (grad_hidden, tokens, norm1),
        [SMEM] + [VMEM] * 7,
        10**7,
        6 * 10**6,
        scratch_shapes=[pltpu.VMEM((span, model), f32)],
    )
    grad_pre, norm_row = lax.optimization_barrier((grad_pre, norm_row))
    grad_expert_in, grad_expert_out = expert_call(
        expert_weight_kernel,
        (struct(expert_in.shape, f32), struct(expert_out.shape, f32)),
        (n_own, n_oth, g_full, act, grad_pre),
        [row_spec, row_spec, kept_spec(model), kept_spec(hidden_units), kept_spec(hidden_units)],
        (in_spec, out_spec),
        2 * unit,
        55 * 10**6,
    )
    weight_rows = exchange(
        call(
            chunk_kernel,
            struct((groups, chunk + 16, model), bf16),
            (weight_rows, norm_row),
            [VMEM] * 2,
            10**7,
            3 * 10**6,
        )
    )
    grad_norm1, grad_query, grad_key, grad_value, grad_output, grad_bias, grad_norm2, grad_router = call(
        unpack_kernel,
        (
            struct((model,), f32),
            struct((inner, model), f32),
            struct((inner, model), f32),
            struct((inner, model), f32),
            struct((inner, model), f32),
            struct((heads, buckets), f32),
            struct((model,), f32),
            struct((experts, model), f32),
        ),
        (weight_rows,),
        [VMEM],
        10**7,
        5 * 10**6,
        scratch_shapes=[pltpu.VMEM((groups * chunk, model), bf16)],
    )
    layer_out = call(
        layer_out_kernel,
        struct((span, model), bf16),
        (place,) + spread(combine(y_rows)) + (hidden,),
        [SMEM] + [VMEM] * 5,
        10**7,
        4 * 10**6,
    )
    return (
        layer_out,
        grad_tokens,
        grad_norm1,
        grad_query.T,
        grad_key.T,
        grad_value.T,
        grad_output,
        grad_bias,
        grad_norm2,
        grad_router.T,
        grad_expert_in,
        grad_expert_out,
    )


def solution(mesh):
    in_specs = (
        P("dp", None),
        P("dp", None),
        P("dp", None),
        P(),
        P(),
        P(None, "tensor"),
        P(None, "tensor"),
        P(None, "tensor"),
        P("tensor", None),
        P("tensor", None),
        P(),
        P(),
        P("dp", None, "tensor"),
        P("dp", "tensor", None),
        P("dp", None),
    )
    out_specs = (
        P("dp", None),
        P("dp", None),
        P(),
        P(None, "tensor"),
        P(None, "tensor"),
        P(None, "tensor"),
        P("tensor", None),
        P("tensor", None),
        P(),
        P(),
        P("dp", None, "tensor"),
        P("dp", "tensor", None),
    )
    return jax.shard_map(
        functools.partial(body, mesh.shape["dp"], mesh.shape["tensor"]),
        mesh=mesh,
        in_specs=in_specs,
        out_specs=out_specs,
        check_vma=False,
    )
```

```python
import functools

import jax
import jax.numpy as jnp
from jax import lax
from jax.experimental import pallas as pl
from jax.experimental.pallas import tpu as pltpu
from jax.sharding import PartitionSpec as P

epsilon = 1e-06
masked_value = -1e30
bf16 = jnp.bfloat16
f32 = jnp.float32
VMEM = pl.BlockSpec(memory_space=pltpu.VMEM)
SMEM = pl.BlockSpec(memory_space=pltpu.SMEM)
vmem_bytes = 56 * 1024 * 1024
expert_vmem_bytes = vmem_bytes
gelu_root = 0.7978845608028654
gelu_cubic = 0.044715


def mm(left, right, left_dim=1, right_dim=0, precision=None):
    return lax.dot_general(
        left,
        right,
        (((left_dim,), (right_dim,)), ((), ())),
        preferred_element_type=f32,
        precision=precision,
    )


def gain_row(ref):
    return ref[...].astype(f32).reshape(1, ref.shape[0])


def iota(shape, dim):
    return lax.broadcasted_iota(jnp.int32, shape, dim)


def call(kernel, out_shape, operands, specs, flops, nbytes, **options):
    return pl.pallas_call(
        kernel,
        out_shape=out_shape,
        in_specs=specs,
        compiler_params=pltpu.CompilerParams(vmem_limit_bytes=vmem_bytes),
        cost_estimate=pl.CostEstimate(flops=flops, bytes_accessed=nbytes, transcendentals=0),
        **options,
    )(*operands)


def half(ref_or_width, which, width):
    return pl.ds(pl.multiple_of(which * width, 128), width)


def route_kernel(place_ref, routes_ref, cotangent_ref, placing_ref, payload_ref, *, experts, capacity):
    tokens = routes_ref.shape[1]
    groups, padded_rows, width = payload_ref.shape
    rows = experts * capacity // groups
    sent = padded_rows - 16
    core = place_ref[0]
    ids = iota((experts, tokens), 0)
    hit = ((routes_ref[0:1, :] == ids) | (routes_ref[1:2, :] == ids)).astype(f32)
    earlier = (iota((tokens, tokens), 0) < iota((tokens, tokens), 1)).astype(bf16)
    rank = mm(hit.astype(bf16), earlier)
    slot = jnp.where(hit > 0.5, rank, -1.0)
    id_sum = jnp.sum(hit * ids.astype(f32), axis=0, keepdims=True)
    id_sum = jnp.broadcast_to(id_sum, (16, tokens)).astype(bf16)
    slot_iota = iota((capacity, tokens), 0).astype(f32)
    for e in range(experts):
        placing_ref[e * capacity : (e + 1) * capacity, :] = (slot[e : e + 1, :] == slot_iota).astype(bf16)
    grad_half = cotangent_ref[:, half(None, core, width)]
    start = 0 if sent == rows else place_ref[2] * sent
    for d in range(groups):
        placed = placing_ref[pl.ds(pl.multiple_of(d * rows + start, 16), sent), :]
        payload_ref[d, 0:sent, :] = mm(placed, grad_half).astype(bf16)
        slot_ids = mm(id_sum, placed, 1, 1).astype(bf16)
        payload_ref[d, sent : sent + 16, :] = jnp.concatenate(
            [slot_ids, jnp.zeros((16, width - sent), bf16)], axis=1
        )


def bucket_rows(rel_bucket_ref, span, buckets):
    offsets = rel_bucket_ref.shape[1]
    backwards = (iota((offsets, span), 0) == span - 1 - iota((offsets, span), 1)).astype(bf16)
    table = jnp.broadcast_to(rel_bucket_ref[...].astype(f32), (16, offsets)).astype(bf16)
    reversed_bucket = mm(table, backwards)[0:1, :]
    return reversed_bucket == iota((buckets, span), 0).astype(f32)


def attention_kernel(
    lengths_ref,
    tokens_ref,
    rel_bucket_ref,
    norm1_ref,
    wq_ref,
    wk_ref,
    wv_ref,
    table_ref,
    attended_ref,
    q_ref,
    k_ref,
    v_ref,
    probs_ref,
):
    span = tokens_ref.shape[0]
    heads, buckets = table_ref.shape
    size = wq_ref.shape[0] // heads
    x = tokens_ref[...].astype(f32)
    r1 = lax.rsqrt(jnp.mean(x * x, axis=1, keepdims=True) + epsilon)
    normed = (x * r1 * gain_row(norm1_ref)).astype(bf16)
    q = mm(normed, wq_ref[...], 1, 1).astype(bf16)
    k = mm(normed, wk_ref[...], 1, 1).astype(bf16)
    v = mm(normed, wv_ref[...], 1, 1).astype(bf16)
    q_ref[...] = q
    k_ref[...] = k
    v_ref[...] = v
    query_index = iota((span, 1), 0)
    key_index = iota((1, span), 1)
    query_segment = jnp.zeros((span, 1), jnp.int32)
    key_segment = jnp.zeros((1, span), jnp.int32)
    end = jnp.int32(0)
    for j in range(lengths_ref.shape[1]):
        end = end + lengths_ref[0, j]
        query_segment = query_segment + (query_index >= end).astype(jnp.int32)
        key_segment = key_segment + (key_index >= end).astype(jnp.int32)
    allowed = (query_segment == key_segment) & (query_index >= key_index)
    indicator = bucket_rows(rel_bucket_ref, span, buckets).astype(bf16)
    bias_rows = mm(table_ref[...], indicator)
    outs = []
    for h in range(heads):
        cut = slice(h * size, (h + 1) * size)
        bias = jnp.broadcast_to(bias_rows[h : h + 1, :], (span, span))
        bias = pltpu.roll(bias, 1, 1, stride=1, stride_axis=0)
        scores = mm(q[:, cut], k[:, cut], 1, 1) * (size**-0.5) + bias
        scores = jnp.where(allowed, scores, masked_value)
        lifted = jnp.exp(scores - jnp.max(scores, axis=1, keepdims=True))
        probs = lifted / jnp.sum(lifted, axis=1, keepdims=True)
        probs = probs.astype(bf16)
        probs_ref[h] = probs
        outs.append(mm(probs, v[:, cut]))
    attended_ref[...] = jnp.concatenate(outs, axis=1).astype(bf16)


def hidden_kernel(
    core_ref,
    tokens_ref,
    a0_ref,
    a1_ref,
    a2_ref,
    a3_ref,
    w0_ref,
    w1_ref,
    w2_ref,
    w3_ref,
    norm2_ref,
    placing_ref,
    hidden_ref,
    *refs,
):
    normed_ref, heads_ref, weights_ref = refs[-3:]
    payload_refs = refs[:-3]
    groups, rows, width = payload_refs[0].shape
    core, far = core_ref[0], core_ref[2]
    parts = ((a0_ref, w0_ref), (a1_ref, w1_ref), (a2_ref, w2_ref), (a3_ref, w3_ref))
    for bits, (a, w) in enumerate(parts):
        index = (far ^ (bits // 2)) * 2 + (core ^ (bits % 2))
        heads_ref[index] = a[...]
        weights_ref[index] = w[...]
    hidden = tokens_ref[...].astype(f32)
    for index in range(4):
        hidden = hidden + mm(heads_ref[index], weights_ref[index])
    hidden_ref[...] = hidden
    r2 = lax.rsqrt(jnp.mean(hidden * hidden, axis=1, keepdims=True) + epsilon)
    normed_ref[...] = (hidden * r2 * gain_row(norm2_ref)).astype(bf16)
    normed_half = normed_ref[:, half(None, core_ref[0], width)]
    parts = len(payload_refs)
    for d in range(groups):
        for part, payload_ref in enumerate(payload_refs):
            start = pl.multiple_of((d * parts + (core_ref[3] ^ part)) * rows, 16)
            payload_ref[d] = mm(placing_ref[pl.ds(start, rows), :], normed_half).astype(bf16)


def merge_rows(ref):
    a, b, c = ref.shape
    return ref[...].reshape(a * b, c)


def whole_rows(even, own, oth):
    return jnp.concatenate([jnp.where(even, own, oth), jnp.where(even, oth, own)], axis=1)


def part_rows(low, rows):
    width = rows.shape[1] // 2
    return jnp.where(low, rows[:, :width], rows[:, width:])


def first_expert(place_ref, part, share):
    return place_ref[1] + (place_ref[3] ^ part) * share


def cotangent_kernel(
    place_ref, ids_ref, own_ref, oth_ref, w_out_ref, back_ref, rows_ref, other_ref, *, part, share
):
    e = pl.program_id(0)
    blocks, capacity, width = own_ref.shape
    rows = blocks * capacity
    experts = other_ref.shape[2]
    ids = ids_ref[:, 0:1, :].astype(f32)
    ids = jnp.broadcast_to(ids, (blocks, capacity, width)).reshape(rows, width)
    lane = iota((rows, width), 1)
    slot = lax.rem(iota((rows, width), 0), capacity)
    id_sum = jnp.sum(jnp.where(lane == e * capacity + slot, ids, 0.0), axis=1, keepdims=True)
    other = id_sum.astype(jnp.int32) - (first_expert(place_ref, part, share) + e)
    other_ref[0] = (iota((rows, experts), 1) == other).astype(bf16)
    g = whole_rows(place_ref[0] == 0, merge_rows(own_ref), merge_rows(oth_ref))
    rows_ref[0] = g
    back_ref[0] = mm(g, w_out_ref[0], 1, 1).astype(bf16)


def expert_grad_kernel(
    place_ref,
    n_own_ref,
    n_oth_ref,
    back_ref,
    other_ref,
    router_ref,
    w_in_ref,
    w_out_ref,
    keep_ref,
    send_ref,
    act_ref,
    pre_ref,
    y_keep_ref,
    y_send_ref,
    coefficient_ref,
    *,
    part,
    share,
):
    per, rows, units = pre_ref.shape
    blocks, _, width = n_own_ref.shape
    capacity = rows // blocks
    experts = router_ref.shape[0]
    core = place_ref[0]
    even = core == 0
    first = first_expert(place_ref, part, share) + pl.program_id(0) * per
    for i in range(per):
        slots = slice(i * capacity, (i + 1) * capacity)
        n = whole_rows(
            even, n_own_ref[:, slots, :].reshape(rows, width), n_oth_ref[:, slots, :].reshape(rows, width)
        )
        is_own = iota((rows, experts), 1) == first + i
        is_other = other_ref[i].astype(f32)
        logits = mm(n, router_ref[...], 1, 1)
        logit_own = jnp.sum(jnp.where(is_own, logits, 0.0), axis=1, keepdims=True)
        logit_other = jnp.sum(is_other * logits, axis=1, keepdims=True)
        peak = jnp.maximum(logit_own, logit_other)
        up_own, up_other = jnp.exp(logit_own - peak), jnp.exp(logit_other - peak)
        gate = up_own / (up_own + up_other)
        grad_gate = jnp.zeros((rows, 1), f32)
        step = 256 if units % 256 == 0 else units
        for start in range(0, units, step):
            cut = slice(start, start + step)
            pre = mm(n, w_in_ref[i, :, cut])
            square = pre * pre
            bend = jnp.tanh(pre * (gelu_root + gelu_root * gelu_cubic * square))
            rise = 0.5 + 0.5 * bend
            act = pre * rise
            slope = rise + act * (1.0 - bend) * (gelu_root + 3.0 * gelu_root * gelu_cubic * square)
            back = gate * back_ref[i, :, cut].astype(f32)
            grad_gate = grad_gate + jnp.sum(act * back, axis=1, keepdims=True)
            act_ref[i, :, cut] = (gate * act).astype(bf16)
            pre_ref[i, :, cut] = (back * slope).astype(bf16)
        grad_logit = grad_gate * (up_other / (up_own + up_other))
        coefficient = (jnp.where(is_own, grad_logit, 0.0) - is_other * grad_logit).astype(bf16)
        coefficient_ref[i] = coefficient
        rows_back = (mm(pre_ref[i], w_in_ref[i], 1, 1) + mm(coefficient, router_ref[...])).astype(bf16)
        y = mm(act_ref[i], w_out_ref[i]).astype(bf16)
        for take, grad_ref, y_ref in ((core == 1, send_ref, y_send_ref), (even, keep_ref, y_keep_ref)):
            grad_ref[:, slots, :] = part_rows(take, rows_back).reshape(blocks, capacity, width)
            y_ref[:, slots, :] = part_rows(take, y).reshape(blocks, capacity, width)


def router_kernel(place_ref, *refs):
    out_ref = refs[-1]
    parts = (len(refs) - 1) // 3
    core = place_ref[0]
    totals = [None, None]
    for part in range(parts):
        n_refs, coefficient_ref = refs[3 * part : 3 * part + 2], refs[3 * part + 2]
        local_experts, rows, _ = coefficient_ref.shape
        groups, _, width = n_refs[0].shape
        capacity = rows // groups
        for which in range(2):
            for i in range(local_experts):
                n = n_refs[which][:, i * capacity : (i + 1) * capacity, :].reshape(rows, width)
                term = mm(coefficient_ref[i], n, 0, 0)
                totals[which] = term if totals[which] is None else totals[which] + term
    out_ref[:, half(None, core, width)] = totals[0]
    out_ref[:, half(None, 1 - core, width)] = totals[1]


def expert_weight_kernel(place_ref, *refs, share):
    grad_in_ref, grad_out_ref = refs[-2:]
    e, j = pl.program_id(0), pl.program_id(1)

    def add(n_own_ref, n_oth_ref, act_ref, pre_ref, g_ref):
        n = whole_rows(place_ref[0] == 0, merge_rows(n_own_ref), merge_rows(n_oth_ref))

        @pl.when(j == 0)
        def _():
            grad_out_ref[0] = mm(act_ref[0], g_ref[0], 0, 0)
            grad_in_ref[0] = mm(n, pre_ref[0], 0, 0)

        @pl.when(j > 0)
        def _():
            grad_out_ref[0] += mm(act_ref[0], g_ref[0], 0, 0)
            grad_in_ref[0] += mm(n, pre_ref[0], 0, 0)

    for part in range((len(refs) - 2) // 5):
        pl.when(e // share == part)(functools.partial(add, *refs[5 * part : 5 * part + 5]))


def combine_kernel(place_ref, placing_ref, rows_ref, *refs):
    out_ref = refs[-1]
    groups, rows, width = rows_ref.shape
    placing = placing_ref[...].reshape(groups * rows, placing_ref.shape[3])
    total = mm(placing, rows_ref[...].reshape(groups * rows, width), 0, 0)
    if len(refs) == 2:
        total = total + refs[0][...]
    out_ref[...] = total.astype(out_ref.dtype)


def attention_back_kernel(
    core_ref,
    z0_ref,
    z1_ref,
    z2_ref,
    z3_ref,
    hidden_ref,
    cotangent_ref,
    tokens_ref,
    norm1_ref,
    norm2_ref,
    wo_ref,
    attended_ref,
    q_ref,
    k_ref,
    v_ref,
    probs_ref,
    rel_bucket_ref,
    grad_router_ref,
    grad_hidden_ref,
    weights_ref,
    low_ref,
    gn_ref,
    all_ref,
):
    span, model = hidden_ref.shape
    heads = probs_ref.shape[0]
    size = q_ref.shape[1] // heads
    inner = q_ref.shape[1]
    width = z0_ref.shape[1]
    core = core_ref[0]
    own = half(None, core, width)
    oth = half(None, 1 - core, width)
    gn_ref[:, own] = z0_ref[...].astype(f32) + z2_ref[...].astype(f32)
    gn_ref[:, oth] = z1_ref[...].astype(f32) + z3_ref[...].astype(f32)
    grad_normed = gn_ref[...]
    hidden = hidden_ref[...]
    r2 = lax.rsqrt(jnp.mean(hidden * hidden, axis=1, keepdims=True) + epsilon)
    weighted = grad_normed * gain_row(norm2_ref)
    inner_mean = jnp.mean(hidden * weighted, axis=1, keepdims=True)
    grad_hidden = cotangent_ref[...].astype(f32) + (r2 * weighted - hidden * (r2 * r2 * r2) * inner_mean)
    grad_hidden_ref[...] = grad_hidden
    grad_norm2 = jnp.sum(grad_normed * hidden * r2, axis=0, keepdims=True)
    branch = grad_hidden.astype(bf16)
    all_ref[3 * inner : 4 * inner, :] = mm(attended_ref[...], branch, 0, 0)
    grad_attended = mm(branch, wo_ref[...], 1, 1).astype(bf16)
    indicator = bucket_rows(rel_bucket_ref, span, 128).astype(f32)
    flip = (iota((span, span), 0) + iota((span, span), 1) == span - 1).astype(bf16)
    q, k, v = q_ref[...], k_ref[...], v_ref[...]
    dq, dk, dv, diagonals = [], [], [], []
    for h in range(heads):
        cut = slice(h * size, (h + 1) * size)
        ga = grad_attended[:, cut]
        dv.append(mm(probs_ref[h], ga, 0, 0))
        probs = probs_ref[h].astype(f32)
        grad_probs = mm(ga, v[:, cut], 1, 1)
        delta = jnp.sum(probs * grad_probs, axis=1, keepdims=True)
        ds = (probs * (grad_probs - delta)).astype(bf16)
        dq.append(mm(ds, k[:, cut]) * (size**-0.5))
        dk.append(mm(ds, q[:, cut], 0, 0) * (size**-0.5))
        rolled = pltpu.roll(mm(flip, ds), 0, 1, stride=1, stride_axis=0)
        diagonals.append(jnp.sum(rolled, axis=0, keepdims=True))
    diagonals = jnp.concatenate(diagonals + [jnp.zeros((8 - heads, span), f32)], axis=0)
    bias = mm(diagonals, indicator, 1, 1, lax.Precision.HIGHEST)
    bias = jnp.concatenate([bias, jnp.zeros((8, model - 128), f32)], axis=1)
    small = jnp.where(iota((8, model), 0) == 7, grad_norm2, bias).astype(bf16)
    x = tokens_ref[...].astype(f32)
    r1 = lax.rsqrt(jnp.mean(x * x, axis=1, keepdims=True) + epsilon)
    normed = (x * r1 * gain_row(norm1_ref)).astype(bf16)
    for j, parts in enumerate((dq, dk, dv)):
        low = jnp.concatenate(parts, axis=1).astype(bf16)
        low_ref[j] = low
        all_ref[j * inner : (j + 1) * inner, :] = mm(low, normed, 0, 0)
    groups, chunk, _ = weights_ref.shape
    count = 4 * inner // groups
    share = grad_router_ref.shape[0] // groups
    weights_ref[:, chunk - 16 :, :] = jnp.zeros((groups, 16, model), bf16)
    for d in range(groups):
        weights_ref[d, 0:count, :] = all_ref[d * count : (d + 1) * count, :].astype(bf16)
        tail = grad_router_ref[d * share : (d + 1) * share, :].astype(bf16)
        weights_ref[d, chunk - 16 : chunk - 16 + share, :] = tail
        if d < 8:
            weights_ref[d, chunk - 8 : chunk - 7, :] = small[d : d + 1, :]


def input_back_kernel(core_ref, low_ref, wq_ref, wk_ref, wv_ref, keep_ref, send_ref, piece_ref):
    width = keep_ref.shape[1]
    core = core_ref[0]
    piece_ref[...] = (
        mm(low_ref[0], wq_ref[...])
        + mm(low_ref[1], wk_ref[...])
        + mm(low_ref[2], wv_ref[...])
    )
    keep_ref[...] = piece_ref[:, half(None, core, width)]
    send_ref[...] = piece_ref[:, half(None, 1 - core, width)].astype(bf16)


def finish_kernel(
    core_ref,
    u0_ref,
    u1_ref,
    u2_ref,
    u3_ref,
    grad_hidden_ref,
    tokens_ref,
    norm1_ref,
    out_ref,
    norm_row_ref,
    gn_ref,
):
    width = u0_ref.shape[1]
    core = core_ref[0]
    gn_ref[:, half(None, core, width)] = u0_ref[...].astype(f32) + u2_ref[...].astype(f32)
    gn_ref[:, half(None, 1 - core, width)] = u1_ref[...].astype(f32) + u3_ref[...].astype(f32)
    x = tokens_ref[...].astype(f32)
    r1 = lax.rsqrt(jnp.mean(x * x, axis=1, keepdims=True) + epsilon)
    grad_normed = gn_ref[...]
    weighted = grad_normed * gain_row(norm1_ref)
    inner_mean = jnp.mean(x * weighted, axis=1, keepdims=True)
    out_ref[...] = grad_hidden_ref[...] + (r1 * weighted - x * (r1 * r1 * r1) * inner_mean)
    row = jnp.sum(grad_normed * x * r1, axis=0, keepdims=True)
    norm_row_ref[...] = jnp.broadcast_to(row, norm_row_ref.shape).astype(bf16)


def chunk_kernel(rows_ref, norm_row_ref, out_ref):
    groups, chunk, model = rows_ref.shape
    total = rows_ref[0].astype(f32)
    for d in range(1, groups):
        total = total + rows_ref[d].astype(f32)
    norm_row = norm_row_ref[...].astype(f32)[0:1, :]
    total = jnp.where(iota((chunk, model), 0) == chunk - 1, norm_row, total).astype(bf16)
    for d in range(groups):
        out_ref[d] = total


def unpack_kernel(
    rows_ref, norm1_ref, wq_ref, wk_ref, wv_ref, wo_ref, bias_ref, norm2_ref, router_ref, all_ref
):
    groups, chunk, _ = rows_ref.shape
    inner = wo_ref.shape[0]
    experts = router_ref.shape[0]
    heads, buckets = bias_ref.shape
    count = 4 * inner // groups
    share = experts // groups
    norm1 = None
    for d in range(groups):
        all_ref[d * count : (d + 1) * count, :] = rows_ref[d, 0:count, :].astype(f32)
        tail = rows_ref[d, chunk - 16 : chunk, :].astype(f32)
        router_ref[d * share : (d + 1) * share, :] = tail[0:share, :]
        if d < heads:
            bias_ref[d : d + 1, :] = tail[8:9, 0:buckets]
        if d == 7:
            norm2_ref[...] = tail[8:9, :].reshape(norm2_ref.shape)
        norm1 = tail[15:16, :] if norm1 is None else norm1 + tail[15:16, :]
    norm1_ref[...] = norm1.reshape(norm1_ref.shape)
    for j, out in enumerate((wq_ref, wk_ref, wv_ref, wo_ref)):
        out[...] = all_ref[j * inner : (j + 1) * inner, :]


def layer_out_kernel(core_ref, y0_ref, y1_ref, y2_ref, y3_ref, hidden_ref, out_ref):
    width = y0_ref.shape[1]
    core = core_ref[0]
    own = half(None, core, width)
    oth = half(None, 1 - core, width)
    out_ref[:, own] = (
        hidden_ref[:, own] + (y0_ref[...].astype(f32) + y2_ref[...].astype(f32))
    ).astype(bf16)
    out_ref[:, oth] = (
        hidden_ref[:, oth] + (y1_ref[...].astype(f32) + y3_ref[...].astype(f32))
    ).astype(bf16)


def struct(shape, dtype):
    return jax.ShapeDtypeStruct(shape, dtype)


def body(
    groups,
    lanes,
    tokens,
    lengths,
    routes,
    rel_bucket,
    norm1,
    w_query,
    w_key,
    w_value,
    output_weight,
    position_bias_table,
    norm2,
    router,
    expert_in,
    expert_out,
    cotangent,
):
    span, model = tokens.shape
    heads, buckets = position_bias_table.shape
    inner = w_query.shape[1]
    experts = router.shape[1]
    local_experts, _, hidden_units = expert_in.shape
    capacity = 2 * routes.shape[1] * span // experts
    rows = local_experts * capacity
    width = model // 2
    rel_bucket = rel_bucket.reshape(1, -1)
    member = lax.axis_index("tensor")
    group = lax.axis_index("dp")
    halves = 2 if local_experts % 2 == 0 else 1
    far = member // 2
    place = jnp.stack([lax.rem(member, 2), group * local_experts, far, far * (halves - 1)])
    place = place.astype(jnp.int32)
    share = local_experts // halves
    sent = rows // halves

    def swap(value, bits):
        return lax.ppermute(value, "tensor", [(i, i ^ bits) for i in range(lanes)])

    def spread(value):
        far = swap(value, 2)
        return value, swap(value, 1), far, swap(far, 1)

    def exchange(value):
        return lax.all_to_all(value, "dp", split_axis=0, concat_axis=0, tiled=True)

    def add_low(left, right):
        return (left.astype(f32) + right.astype(f32)).astype(bf16)

    placing, grad_payload = call(
        functools.partial(route_kernel, experts=experts, capacity=capacity),
        (
            struct((experts * capacity, span), bf16),
            struct((groups, sent + 16, width), bf16),
        ),
        (place, routes.T, cotangent),
        [SMEM, VMEM, VMEM],
        3 * 10**9,
        6 * 10**6,
    )
    g_rows = [exchange(grad_payload)]
    output_weights = spread(output_weight)
    attended, q, k, v, probs = call(
        attention_kernel,
        (
            struct((span, inner), bf16),
            struct((span, inner), bf16),
            struct((span, inner), bf16),
            struct((span, inner), bf16),
            struct((heads, span, span), bf16),
        ),
        (lengths, tokens, rel_bucket, norm1, w_query.T, w_key.T, w_value.T, position_bias_table),
        [SMEM] + [VMEM] * 7,
        6 * 10**9,
        8 * 10**6,
    )
    attended_all = spread(attended)
    hidden, *payloads = call(
        hidden_kernel,
        (struct((span, model), f32),) + (struct((groups, sent, width), bf16),) * halves,
        (place, tokens) + attended_all + output_weights + (norm2, placing),
        [SMEM] + [VMEM] * 11,
        2 * 10**9,
        8 * 10**6,
        scratch_shapes=[
            pltpu.VMEM((span, model), bf16),
            pltpu.VMEM((4, span, inner), bf16),
            pltpu.VMEM((4, inner, model), bf16),
        ],
    )
    payloads[0], g_rows[0] = lax.optimization_barrier((payloads[0], g_rows[0]))
    if halves == 2:
        g_rows.append(swap(g_rows[0], 2))
    n_owns = [exchange(payloads[0])]

    blocks = min(groups, 8)
    steps = groups // blocks
    block_rows = blocks * capacity
    row_spec = pl.BlockSpec((blocks, capacity, width), lambda e, j, p: (j, e, 0))

    ids_spec = pl.BlockSpec((blocks, 16, width), lambda e, j, p: (j, sent // 16, 0))

    def kept_spec(columns):
        return pl.BlockSpec((1, block_rows, columns), lambda e, j, p: (e, j, 0))

    def ordered(e, p):
        return (p[3] ^ (e // share)) * share + lax.rem(e, share)

    in_spec = pl.BlockSpec((1, model, hidden_units), lambda e, j, p: (ordered(e, p), 0, 0))
    out_spec = pl.BlockSpec((1, hidden_units, model), lambda e, j, p: (ordered(e, p), 0, 0))
    router_spec = pl.BlockSpec((experts, model), lambda e, j, p: (0, 0))
    unit = 2 * groups * rows * model * hidden_units

    def expert_call(kernel, out_shape, operands, in_specs, out_specs, flops, nbytes, grid=None):
        return pl.pallas_call(
            kernel,
            out_shape=out_shape,
            grid_spec=pltpu.PrefetchScalarGridSpec(
                num_scalar_prefetch=1,
                grid=grid or (local_experts, steps),
                in_specs=in_specs,
                out_specs=out_specs,
            ),
            compiler_params=pltpu.CompilerParams(vmem_limit_bytes=expert_vmem_bytes),
            cost_estimate=pl.CostEstimate(flops=flops, bytes_accessed=nbytes, transcendentals=0),
        )(place, *operands)

    which = range(halves)
    n_oths = [None] * halves
    back_rows, y_rows, kept = [None] * halves, [None] * halves, [None] * halves
    part_struct = struct((groups, sent, width), bf16)

    def weight_spec(weight, part):
        return pl.BlockSpec((1,) + weight.shape[1:], lambda e, j, p: ((p[3] ^ part) * share + e, 0, 0))

    def part_kept(columns):
        return struct((share, groups * capacity, columns), bf16)

    def multiply_cotangent(part):
        g_own = g_rows[part]
        return expert_call(
            functools.partial(cotangent_kernel, part=part, share=share),
            (part_kept(hidden_units), part_kept(model), part_kept(experts)),
            (g_own, g_own, swap(g_own, 1), expert_out),
            [ids_spec, row_spec, row_spec, weight_spec(expert_out, part)],
            (kept_spec(hidden_units), kept_spec(model), kept_spec(experts)),
            unit // halves,
            20 * 10**6 // halves,
            grid=(share, steps),
        )

    backs = [multiply_cotangent(0)] + [None] * (halves - 1)
    if halves == 2:
        later, n_owns[0], back = lax.optimization_barrier((payloads[1], n_owns[0], backs[0][0]))
        backs[0] = (back,) + tuple(backs[0][1:])
        n_owns.append(exchange(later))
    for part in which:
        back, g_full, other = backs[part]
        n_oths[part] = swap(n_owns[part], 1)
        if part + 1 < halves:
            n_oths[part], g_rows[1] = lax.optimization_barrier((n_oths[part], g_rows[1]))
            backs[1] = multiply_cotangent(1)
        keep, send, act, grad_pre, y_keep, y_send, coefficient = expert_call(
            functools.partial(expert_grad_kernel, part=part, share=share),
            (part_struct, part_struct, part_kept(hidden_units), part_kept(hidden_units))
            + (part_struct, part_struct, part_kept(experts)),
            (n_owns[part], n_oths[part], back, other, router.T, expert_in, expert_out),
            [row_spec, row_spec, kept_spec(hidden_units), kept_spec(experts), router_spec]
            + [weight_spec(expert_in, part), weight_spec(expert_out, part)],
            (row_spec, row_spec, kept_spec(hidden_units), kept_spec(hidden_units))
            + (row_spec, row_spec, kept_spec(experts)),
            3 * unit // halves,
            35 * 10**6 // halves,
            grid=(share, steps),
        )
        kept[part] = (n_owns[part], n_oths[part], act, grad_pre, g_full, coefficient)
        total = add_low(keep, swap(send, 1))
        if part + 1 < halves:
            total, n_owns[1], other = lax.optimization_barrier((total, n_owns[1], backs[1][2]))
            backs[1] = tuple(backs[1][:2]) + (other,)
        elif part > 0:
            total, back_rows[0] = lax.optimization_barrier((total, back_rows[0]))
        total, y_send = lax.optimization_barrier((total, y_send))
        back_rows[part] = exchange(total)
        y_rows[part] = (y_keep, y_send)
    y_rows = [add_low(y_keep, swap(y_send, 1)) for y_keep, y_send in y_rows]
    last, y_rows[-1] = lax.optimization_barrier((kept[-1][5], y_rows[-1]))
    kept[-1] = kept[-1][:5] + (last,)
    if halves == 2:
        y_near, y_far = y_rows[0], swap(y_rows[1], 2)
    def combine(value, part, before=None, dtype=bf16):
        parted = placing.reshape(groups, halves, sent, span)
        out_spec = pl.BlockSpec((span, width), lambda i, p: (0, 0))
        placing_spec = pl.BlockSpec(
            (groups, 1, sent, span), lambda i, p: (0, p[3] ^ part, 0, 0)
        )
        rows_spec = pl.BlockSpec((groups, sent, width), lambda i, p: (0, 0, 0))
        return pl.pallas_call(
            combine_kernel,
            out_shape=struct((span, width), dtype),
            grid_spec=pltpu.PrefetchScalarGridSpec(
                num_scalar_prefetch=1,
                grid=(1,),
                in_specs=[placing_spec, rows_spec] + [out_spec] * (before is not None),
                out_specs=out_spec,
            ),
            compiler_params=pltpu.CompilerParams(vmem_limit_bytes=vmem_bytes),
            cost_estimate=pl.CostEstimate(flops=10**9, bytes_accessed=4 * 10**6, transcendentals=0),
        )(place, parted, value, *([] if before is None else [before]))

    grad_router = call(
        router_kernel,
        struct((experts, model), f32),
        (place,) + sum([(a, b, c) for a, b, _, _, _, c in kept], ()),
        [SMEM] + [VMEM] * (3 * halves),
        10**9,
        4 * 10**6,
    )
    before = None
    if halves == 2:
        before = combine(back_rows[0], 0, None, f32)
        grad_router, before = lax.optimization_barrier((grad_router, before))
    grad_router = grad_router + swap(grad_router, 1)
    grad_router = grad_router.astype(bf16)
    grad_router = grad_router.astype(f32) + swap(grad_router, 2).astype(f32)


    if halves == 2:
        back_rows[1], before = lax.optimization_barrier((back_rows[1], before))
        z = combine(back_rows[1], 1, before)
        z, y_far = lax.optimization_barrier((z, y_far))
        y_rows = add_low(y_near, y_far)
    else:
        z = combine(back_rows[0], 0)
        y_rows = y_rows[0]
    y_rows = exchange(y_rows)
    z = spread(z)
    chunk = -(-4 * inner // (16 * groups)) * 16 + 16
    grad_hidden, weights, low = call(
        attention_back_kernel,
        (
            struct((span, model), f32),
            struct((groups, chunk, model), bf16),
            struct((3, span, inner), bf16),
        ),
        (place,)
        + z
        + (hidden, cotangent, tokens, norm1, norm2, output_weight)
        + (attended, q, k, v, probs, rel_bucket, grad_router),
        [SMEM] + [VMEM] * 17,
        10 * 10**9,
        14 * 10**6,
        scratch_shapes=[pltpu.VMEM((span, model), f32), pltpu.VMEM((4 * inner, model), f32)],
    )
    weights, y_rows = lax.optimization_barrier((weights, y_rows))
    weight_rows = exchange(weights)
    piece_keep, piece_send = call(
        input_back_kernel,
        (struct((span, width), f32), struct((span, width), bf16)),
        (place, low, w_query.T, w_key.T, w_value.T),
        [SMEM] + [VMEM] * 4,
        10**9,
        4 * 10**6,
        scratch_shapes=[pltpu.VMEM((span, model), f32)],
    )
    piece = add_low(piece_keep, swap(piece_send, 1))
    grad_tokens, norm_row = call(
        finish_kernel,
        (struct((span, model), f32), struct((16, model), bf16)),
        (place,) + spread(piece) + (grad_hidden, tokens, norm1),
        [SMEM] + [VMEM] * 7,
        10**7,
        6 * 10**6,
        scratch_shapes=[pltpu.VMEM((span, model), f32)],
    )
    grad_pre, norm_row = lax.optimization_barrier((grad_pre, norm_row))
    operands, specs = (), []
    for part in which:
        if part == halves - 1:
            kept[part] = kept[part][:3] + (grad_pre,) + kept[part][4:]

        def near_index(e, first=part * share):
            return jnp.clip(e - first, 0, share - 1)

        operands = operands + kept[part][:5]
        for _ in range(2):
            specs.append(
                pl.BlockSpec((blocks, capacity, width), lambda e, j, p, f=near_index: (j, f(e), 0))
            )
        for columns in (hidden_units, hidden_units, model):
            specs.append(
                pl.BlockSpec((1, block_rows, columns), lambda e, j, p, f=near_index: (f(e), j, 0))
            )
    grad_expert_in, grad_expert_out = expert_call(
        functools.partial(expert_weight_kernel, share=share),
        (struct(expert_in.shape, f32), struct(expert_out.shape, f32)),
        operands,
        specs,
        (in_spec, out_spec),
        2 * unit,
        55 * 10**6,
    )
    norm_row, y_rows = lax.optimization_barrier((norm_row, y_rows))
    y_part = combine(y_rows, 0)
    weight_rows, y_part = lax.optimization_barrier((weight_rows, y_part))
    weight_rows = exchange(
        call(
            chunk_kernel,
            struct((groups, chunk, model), bf16),
            (weight_rows, norm_row),
            [VMEM] * 2,
            10**7,
            3 * 10**6,
        )
    )
    grad_norm1, grad_query, grad_key, grad_value, grad_output, grad_bias, grad_norm2, grad_router = call(
        unpack_kernel,
        (
            struct((model,), f32),
            struct((inner, model), f32),
            struct((inner, model), f32),
            struct((inner, model), f32),
            struct((inner, model), f32),
            struct((heads, buckets), f32),
            struct((model,), f32),
            struct((experts, model), f32),
        ),
        (weight_rows,),
        [VMEM],
        10**7,
        5 * 10**6,
        scratch_shapes=[pltpu.VMEM((4 * inner, model), f32)],
    )
    layer_out = call(
        layer_out_kernel,
        struct((span, model), bf16),
        (place,) + spread(y_part) + (hidden,),
        [SMEM] + [VMEM] * 5,
        10**7,
        4 * 10**6,
    )
    return (
        layer_out,
        grad_tokens,
        grad_norm1,
        grad_query.T,
        grad_key.T,
        grad_value.T,
        grad_output,
        grad_bias,
        grad_norm2,
        grad_router.T,
        grad_expert_in,
        grad_expert_out,
    )


def solution(mesh):
    in_specs = (
        P("dp", None),
        P("dp", None),
        P("dp", None),
        P(),
        P(),
        P(None, "tensor"),
        P(None, "tensor"),
        P(None, "tensor"),
        P("tensor", None),
        P("tensor", None),
        P(),
        P(),
        P("dp", None, "tensor"),
        P("dp", "tensor", None),
        P("dp", None),
    )
    out_specs = (
        P("dp", None),
        P("dp", None),
        P(),
        P(None, "tensor"),
        P(None, "tensor"),
        P(None, "tensor"),
        P("tensor", None),
        P("tensor", None),
        P(),
        P(),
        P("dp", None, "tensor"),
        P("dp", "tensor", None),
    )
    return jax.shard_map(
        functools.partial(body, mesh.shape["dp"], mesh.shape["tensor"]),
        mesh=mesh,
        in_specs=in_specs,
        out_specs=out_specs,
        check_vma=False,
    )
```

```python
import functools

import jax
import jax.numpy as jnp
from jax import lax
from jax.experimental import pallas as pl
from jax.experimental.pallas import tpu as pltpu
from jax.sharding import PartitionSpec as P

epsilon = 1e-06
masked_value = -1e30
bf16 = jnp.bfloat16
f32 = jnp.float32
VMEM = pl.BlockSpec(memory_space=pltpu.VMEM)
SMEM = pl.BlockSpec(memory_space=pltpu.SMEM)
vmem_bytes = 56 * 1024 * 1024
expert_vmem_bytes = vmem_bytes
gelu_root = 0.7978845608028654
gelu_cubic = 0.044715


def mm(left, right, left_dim=1, right_dim=0, precision=None):
    return lax.dot_general(
        left,
        right,
        (((left_dim,), (right_dim,)), ((), ())),
        preferred_element_type=f32,
        precision=precision,
    )


def gain_row(ref):
    return ref[...].astype(f32).reshape(1, ref.shape[0])


def iota(shape, dim):
    return lax.broadcasted_iota(jnp.int32, shape, dim)


def call(kernel, out_shape, operands, specs, flops, nbytes, **options):
    return pl.pallas_call(
        kernel,
        out_shape=out_shape,
        in_specs=specs,
        compiler_params=pltpu.CompilerParams(vmem_limit_bytes=vmem_bytes),
        cost_estimate=pl.CostEstimate(flops=flops, bytes_accessed=nbytes, transcendentals=0),
        **options,
    )(*operands)


def half(ref_or_width, which, width):
    return pl.ds(pl.multiple_of(which * width, 128), width)


def route_kernel(place_ref, routes_ref, cotangent_ref, placing_ref, payload_ref, *, experts, capacity):
    tokens = routes_ref.shape[1]
    groups, padded_rows, width = payload_ref.shape
    rows = experts * capacity // groups
    sent = padded_rows - 16
    core = place_ref[0]
    ids = iota((experts, tokens), 0)
    hit = ((routes_ref[0:1, :] == ids) | (routes_ref[1:2, :] == ids)).astype(f32)
    earlier = (iota((tokens, tokens), 0) < iota((tokens, tokens), 1)).astype(bf16)
    rank = mm(hit.astype(bf16), earlier)
    slot = jnp.where(hit > 0.5, rank, -1.0)
    id_sum = jnp.sum(hit * ids.astype(f32), axis=0, keepdims=True)
    id_sum = jnp.broadcast_to(id_sum, (16, tokens)).astype(bf16)
    slot_iota = iota((capacity, tokens), 0).astype(f32)
    for e in range(experts):
        placing_ref[e * capacity : (e + 1) * capacity, :] = (slot[e : e + 1, :] == slot_iota).astype(bf16)
    grad_half = cotangent_ref[:, half(None, core, width)]
    start = 0 if sent == rows else place_ref[2] * sent
    for d in range(groups):
        placed = placing_ref[pl.ds(pl.multiple_of(d * rows + start, 16), sent), :]
        payload_ref[d, 0:sent, :] = mm(placed, grad_half).astype(bf16)
        slot_ids = mm(id_sum, placed, 1, 1).astype(bf16)
        payload_ref[d, sent : sent + 16, :] = jnp.concatenate(
            [slot_ids, jnp.zeros((16, width - sent), bf16)], axis=1
        )


def bucket_rows(rel_bucket_ref, span, buckets):
    offsets = rel_bucket_ref.shape[1]
    backwards = (iota((offsets, span), 0) == span - 1 - iota((offsets, span), 1)).astype(bf16)
    table = jnp.broadcast_to(rel_bucket_ref[...].astype(f32), (16, offsets)).astype(bf16)
    reversed_bucket = mm(table, backwards)[0:1, :]
    return reversed_bucket == iota((buckets, span), 0).astype(f32)


def attention_kernel(
    lengths_ref,
    tokens_ref,
    rel_bucket_ref,
    norm1_ref,
    wq_ref,
    wk_ref,
    wv_ref,
    table_ref,
    attended_ref,
    q_ref,
    k_ref,
    v_ref,
    probs_ref,
):
    span = tokens_ref.shape[0]
    heads, buckets = table_ref.shape
    size = wq_ref.shape[0] // heads
    x = tokens_ref[...].astype(f32)
    r1 = lax.rsqrt(jnp.mean(x * x, axis=1, keepdims=True) + epsilon)
    normed = (x * r1 * gain_row(norm1_ref)).astype(bf16)
    q = mm(normed, wq_ref[...], 1, 1).astype(bf16)
    k = mm(normed, wk_ref[...], 1, 1).astype(bf16)
    v = mm(normed, wv_ref[...], 1, 1).astype(bf16)
    q_ref[...] = q
    k_ref[...] = k
    v_ref[...] = v
    query_index = iota((span, 1), 0)
    key_index = iota((1, span), 1)
    query_segment = jnp.zeros((span, 1), jnp.int32)
    key_segment = jnp.zeros((1, span), jnp.int32)
    end = jnp.int32(0)
    for j in range(lengths_ref.shape[1]):
        end = end + lengths_ref[0, j]
        query_segment = query_segment + (query_index >= end).astype(jnp.int32)
        key_segment = key_segment + (key_index >= end).astype(jnp.int32)
    allowed = (query_segment == key_segment) & (query_index >= key_index)
    indicator = bucket_rows(rel_bucket_ref, span, buckets).astype(bf16)
    bias_rows = mm(table_ref[...], indicator)
    outs = []
    for h in range(heads):
        cut = slice(h * size, (h + 1) * size)
        bias = jnp.broadcast_to(bias_rows[h : h + 1, :], (span, span))
        bias = pltpu.roll(bias, 1, 1, stride=1, stride_axis=0)
        scores = mm(q[:, cut], k[:, cut], 1, 1) * (size**-0.5) + bias
        scores = jnp.where(allowed, scores, masked_value)
        lifted = jnp.exp(scores - jnp.max(scores, axis=1, keepdims=True))
        probs = lifted / jnp.sum(lifted, axis=1, keepdims=True)
        probs = probs.astype(bf16)
        probs_ref[h] = probs
        outs.append(mm(probs, v[:, cut]))
    attended_ref[...] = jnp.concatenate(outs, axis=1).astype(bf16)


def hidden_kernel(
    core_ref,
    tokens_ref,
    a0_ref,
    a1_ref,
    a2_ref,
    a3_ref,
    w0_ref,
    w1_ref,
    w2_ref,
    w3_ref,
    norm2_ref,
    placing_ref,
    hidden_ref,
    *refs,
):
    normed_ref, heads_ref, weights_ref = refs[-3:]
    payload_refs = refs[:-3]
    groups, rows, width = payload_refs[0].shape
    core, far = core_ref[0], core_ref[2]
    parts = ((a0_ref, w0_ref), (a1_ref, w1_ref), (a2_ref, w2_ref), (a3_ref, w3_ref))
    for bits, (a, w) in enumerate(parts):
        index = (far ^ (bits // 2)) * 2 + (core ^ (bits % 2))
        heads_ref[index] = a[...]
        weights_ref[index] = w[...]
    hidden = tokens_ref[...].astype(f32)
    for index in range(4):
        hidden = hidden + mm(heads_ref[index], weights_ref[index])
    hidden_ref[...] = hidden
    r2 = lax.rsqrt(jnp.mean(hidden * hidden, axis=1, keepdims=True) + epsilon)
    normed_ref[...] = (hidden * r2 * gain_row(norm2_ref)).astype(bf16)
    normed_half = normed_ref[:, half(None, core_ref[0], width)]
    parts = len(payload_refs)
    for d in range(groups):
        start = d * parts * rows
        placed = mm(placing_ref[start : start + parts * rows, :], normed_half).astype(bf16)
        if parts == 1:
            payload_refs[0][d] = placed
        else:
            first = core_ref[3] == 0
            payload_refs[0][d] = jnp.where(first, placed[:rows], placed[rows:])
            payload_refs[1][d] = jnp.where(first, placed[rows:], placed[:rows])


def merge_rows(ref):
    a, b, c = ref.shape
    return ref[...].reshape(a * b, c)


def whole_rows(even, own, oth):
    return jnp.concatenate([jnp.where(even, own, oth), jnp.where(even, oth, own)], axis=1)


def part_rows(low, rows):
    width = rows.shape[1] // 2
    return jnp.where(low, rows[:, :width], rows[:, width:])


def first_expert(place_ref, part, share):
    return place_ref[1] + (place_ref[3] ^ part) * share


def cotangent_kernel(
    place_ref, ids_ref, own_ref, oth_ref, w_out_ref, back_ref, rows_ref, other_ref, *, part, share
):
    e = pl.program_id(0)
    blocks, capacity, width = own_ref.shape
    rows = blocks * capacity
    experts = other_ref.shape[2]
    ids = ids_ref[:, 0:1, :].astype(f32)
    ids = jnp.broadcast_to(ids, (blocks, capacity, width)).reshape(rows, width)
    lane = iota((rows, width), 1)
    slot = lax.rem(iota((rows, width), 0), capacity)
    id_sum = jnp.sum(jnp.where(lane == e * capacity + slot, ids, 0.0), axis=1, keepdims=True)
    other = id_sum.astype(jnp.int32) - (first_expert(place_ref, part, share) + e)
    other_ref[0] = (iota((rows, experts), 1) == other).astype(bf16)
    g = whole_rows(place_ref[0] == 0, merge_rows(own_ref), merge_rows(oth_ref))
    rows_ref[0] = g
    back_ref[0] = mm(g, w_out_ref[0], 1, 1).astype(bf16)


def expert_grad_kernel(
    place_ref,
    n_own_ref,
    n_oth_ref,
    back_ref,
    other_ref,
    router_ref,
    w_in_ref,
    w_out_ref,
    keep_ref,
    send_ref,
    act_ref,
    pre_ref,
    y_keep_ref,
    y_send_ref,
    coefficient_ref,
    *,
    part,
    share,
):
    per, rows, units = pre_ref.shape
    blocks, _, width = n_own_ref.shape
    capacity = rows // blocks
    experts = router_ref.shape[0]
    core = place_ref[0]
    even = core == 0
    first = first_expert(place_ref, part, share) + pl.program_id(0) * per
    for i in range(per):
        slots = slice(i * capacity, (i + 1) * capacity)
        n = whole_rows(
            even, n_own_ref[:, slots, :].reshape(rows, width), n_oth_ref[:, slots, :].reshape(rows, width)
        )
        is_own = iota((rows, experts), 1) == first + i
        is_other = other_ref[i].astype(f32)
        logits = mm(n, router_ref[...], 1, 1)
        logit_own = jnp.sum(jnp.where(is_own, logits, 0.0), axis=1, keepdims=True)
        logit_other = jnp.sum(is_other * logits, axis=1, keepdims=True)
        peak = jnp.maximum(logit_own, logit_other)
        up_own, up_other = jnp.exp(logit_own - peak), jnp.exp(logit_other - peak)
        gate = up_own / (up_own + up_other)
        grad_gate = jnp.zeros((rows, 1), f32)
        step = 256 if units % 256 == 0 else units
        for start in range(0, units, step):
            cut = slice(start, start + step)
            pre = mm(n, w_in_ref[i, :, cut])
            square = pre * pre
            bend = jnp.tanh(pre * (gelu_root + gelu_root * gelu_cubic * square))
            rise = 0.5 + 0.5 * bend
            act = pre * rise
            slope = rise + act * (1.0 - bend) * (gelu_root + 3.0 * gelu_root * gelu_cubic * square)
            back = gate * back_ref[i, :, cut].astype(f32)
            grad_gate = grad_gate + jnp.sum(act * back, axis=1, keepdims=True)
            act_ref[i, :, cut] = (gate * act).astype(bf16)
            pre_ref[i, :, cut] = (back * slope).astype(bf16)
        grad_logit = grad_gate * (up_other / (up_own + up_other))
        coefficient = (jnp.where(is_own, grad_logit, 0.0) - is_other * grad_logit).astype(bf16)
        coefficient_ref[i] = coefficient
        rows_back = (mm(pre_ref[i], w_in_ref[i], 1, 1) + mm(coefficient, router_ref[...])).astype(bf16)
        y = mm(act_ref[i], w_out_ref[i]).astype(bf16)
        for take, grad_ref, y_ref in ((core == 1, send_ref, y_send_ref), (even, keep_ref, y_keep_ref)):
            grad_ref[:, slots, :] = part_rows(take, rows_back).reshape(blocks, capacity, width)
            y_ref[:, slots, :] = part_rows(take, y).reshape(blocks, capacity, width)


def router_kernel(place_ref, *refs):
    out_ref = refs[-1]
    parts = (len(refs) - 1) // 3
    core = place_ref[0]
    totals = [None, None]
    for part in range(parts):
        n_refs, coefficient_ref = refs[3 * part : 3 * part + 2], refs[3 * part + 2]
        local_experts, rows, _ = coefficient_ref.shape
        groups, _, width = n_refs[0].shape
        capacity = rows // groups
        for which in range(2):
            for i in range(local_experts):
                n = n_refs[which][:, i * capacity : (i + 1) * capacity, :].reshape(rows, width)
                term = mm(coefficient_ref[i], n, 0, 0)
                totals[which] = term if totals[which] is None else totals[which] + term
    out_ref[:, half(None, core, width)] = totals[0]
    out_ref[:, half(None, 1 - core, width)] = totals[1]


def expert_weight_kernel(place_ref, *refs, share):
    grad_in_ref, grad_out_ref = refs[-2:]
    e, j = pl.program_id(0), pl.program_id(1)

    def add(n_own_ref, n_oth_ref, act_ref, pre_ref, g_ref):
        n = whole_rows(place_ref[0] == 0, merge_rows(n_own_ref), merge_rows(n_oth_ref))

        @pl.when(j == 0)
        def _():
            grad_out_ref[0] = mm(act_ref[0], g_ref[0], 0, 0)
            grad_in_ref[0] = mm(n, pre_ref[0], 0, 0)

        @pl.when(j > 0)
        def _():
            grad_out_ref[0] += mm(act_ref[0], g_ref[0], 0, 0)
            grad_in_ref[0] += mm(n, pre_ref[0], 0, 0)

    for part in range((len(refs) - 2) // 5):
        pl.when(e // share == part)(functools.partial(add, *refs[5 * part : 5 * part + 5]))


def combine_kernel(place_ref, placing_ref, rows_ref, *refs, before):
    out_ref = refs[-1]
    groups, rows, width = rows_ref.shape
    placing = placing_ref[...].reshape(groups * rows, placing_ref.shape[3])
    total = mm(placing, rows_ref[...].reshape(groups * rows, width), 0, 0)
    if before:
        total = total + refs[0][...]
    span = total.shape[0]
    out_ref[0:span, :] = total.astype(out_ref.dtype)
    if len(refs) > 1 + before:
        router_ref = refs[before]
        experts = router_ref.shape[0]
        out_ref[span : span + experts, :] = router_ref[:, :width].astype(out_ref.dtype)
        out_ref[span + experts : span + 2 * experts, :] = router_ref[:, width:].astype(out_ref.dtype)


def attention_back_kernel(
    core_ref,
    z0_ref,
    z1_ref,
    z2_ref,
    z3_ref,
    hidden_ref,
    cotangent_ref,
    tokens_ref,
    norm1_ref,
    norm2_ref,
    wo_ref,
    attended_ref,
    q_ref,
    k_ref,
    v_ref,
    probs_ref,
    rel_bucket_ref,
    grad_hidden_ref,
    weights_ref,
    low_ref,
    gn_ref,
    all_ref,
):
    span, model = hidden_ref.shape
    heads = probs_ref.shape[0]
    size = q_ref.shape[1] // heads
    inner = q_ref.shape[1]
    width = z0_ref.shape[1]
    core = core_ref[0]
    own = half(None, core, width)
    oth = half(None, 1 - core, width)
    gn_ref[:, own] = z0_ref[0:span, :].astype(f32) + z2_ref[0:span, :].astype(f32)
    gn_ref[:, oth] = z1_ref[0:span, :].astype(f32) + z3_ref[0:span, :].astype(f32)
    below = [r[span:, :].astype(f32) for r in (z0_ref, z1_ref, z2_ref, z3_ref)]
    router = (below[0] + below[1]) + (below[2] + below[3])
    experts = router.shape[0] // 2
    router = jnp.concatenate([router[:experts], router[experts:]], axis=1).astype(bf16)
    grad_normed = gn_ref[...]
    hidden = hidden_ref[...]
    r2 = lax.rsqrt(jnp.mean(hidden * hidden, axis=1, keepdims=True) + epsilon)
    weighted = grad_normed * gain_row(norm2_ref)
    inner_mean = jnp.mean(hidden * weighted, axis=1, keepdims=True)
    grad_hidden = cotangent_ref[...].astype(f32) + (r2 * weighted - hidden * (r2 * r2 * r2) * inner_mean)
    grad_hidden_ref[...] = grad_hidden
    grad_norm2 = jnp.sum(grad_normed * hidden * r2, axis=0, keepdims=True)
    branch = grad_hidden.astype(bf16)
    all_ref[3 * inner : 4 * inner, :] = mm(attended_ref[...], branch, 0, 0)
    grad_attended = mm(branch, wo_ref[...], 1, 1).astype(bf16)
    indicator = bucket_rows(rel_bucket_ref, span, 128).astype(f32)
    flip = (iota((span, span), 0) + iota((span, span), 1) == span - 1).astype(bf16)
    q, k, v = q_ref[...], k_ref[...], v_ref[...]
    dq, dk, dv, diagonals = [], [], [], []
    for h in range(heads):
        cut = slice(h * size, (h + 1) * size)
        ga = grad_attended[:, cut]
        dv.append(mm(probs_ref[h], ga, 0, 0))
        probs = probs_ref[h].astype(f32)
        grad_probs = mm(ga, v[:, cut], 1, 1)
        delta = jnp.sum(probs * grad_probs, axis=1, keepdims=True)
        ds = (probs * (grad_probs - delta)).astype(bf16)
        dq.append(mm(ds, k[:, cut]) * (size**-0.5))
        dk.append(mm(ds, q[:, cut], 0, 0) * (size**-0.5))
        rolled = pltpu.roll(mm(flip, ds), 0, 1, stride=1, stride_axis=0)
        diagonals.append(jnp.sum(rolled, axis=0, keepdims=True))
    diagonals = jnp.concatenate(diagonals + [jnp.zeros((8 - heads, span), f32)], axis=0)
    bias = mm(diagonals, indicator, 1, 1, lax.Precision.HIGHEST)
    bias = jnp.concatenate([bias, jnp.zeros((8, model - 128), f32)], axis=1)
    small = jnp.where(iota((8, model), 0) == 7, grad_norm2, bias).astype(bf16)
    x = tokens_ref[...].astype(f32)
    r1 = lax.rsqrt(jnp.mean(x * x, axis=1, keepdims=True) + epsilon)
    normed = (x * r1 * gain_row(norm1_ref)).astype(bf16)
    for j, parts in enumerate((dq, dk, dv)):
        low = jnp.concatenate(parts, axis=1).astype(bf16)
        low_ref[j] = low
        all_ref[j * inner : (j + 1) * inner, :] = mm(low, normed, 0, 0)
    groups, chunk, _ = weights_ref.shape
    count = 4 * inner // groups
    share = experts // groups
    weights_ref[:, chunk - 16 :, :] = jnp.zeros((groups, 16, model), bf16)
    for d in range(groups):
        weights_ref[d, 0:count, :] = all_ref[d * count : (d + 1) * count, :].astype(bf16)
        weights_ref[d, chunk - 16 : chunk - 16 + share, :] = router[d * share : (d + 1) * share, :]
        if d < 8:
            weights_ref[d, chunk - 8 : chunk - 7, :] = small[d : d + 1, :]


def input_back_kernel(core_ref, low_ref, wq_ref, wk_ref, wv_ref, keep_ref, send_ref, piece_ref):
    width = keep_ref.shape[1]
    core = core_ref[0]
    piece_ref[...] = (
        mm(low_ref[0], wq_ref[...])
        + mm(low_ref[1], wk_ref[...])
        + mm(low_ref[2], wv_ref[...])
    )
    keep_ref[...] = piece_ref[:, half(None, core, width)]
    send_ref[...] = piece_ref[:, half(None, 1 - core, width)].astype(bf16)


def finish_kernel(
    core_ref,
    u0_ref,
    u1_ref,
    u2_ref,
    u3_ref,
    grad_hidden_ref,
    tokens_ref,
    norm1_ref,
    out_ref,
    norm_row_ref,
    gn_ref,
):
    width = u0_ref.shape[1]
    core = core_ref[0]
    gn_ref[:, half(None, core, width)] = u0_ref[...].astype(f32) + u2_ref[...].astype(f32)
    gn_ref[:, half(None, 1 - core, width)] = u1_ref[...].astype(f32) + u3_ref[...].astype(f32)
    x = tokens_ref[...].astype(f32)
    r1 = lax.rsqrt(jnp.mean(x * x, axis=1, keepdims=True) + epsilon)
    grad_normed = gn_ref[...]
    weighted = grad_normed * gain_row(norm1_ref)
    inner_mean = jnp.mean(x * weighted, axis=1, keepdims=True)
    out_ref[...] = grad_hidden_ref[...] + (r1 * weighted - x * (r1 * r1 * r1) * inner_mean)
    row = jnp.sum(grad_normed * x * r1, axis=0, keepdims=True)
    norm_row_ref[...] = jnp.broadcast_to(row, norm_row_ref.shape).astype(bf16)


def chunk_kernel(rows_ref, norm_row_ref, out_ref):
    groups, chunk, model = rows_ref.shape
    total = rows_ref[0].astype(f32)
    for d in range(1, groups):
        total = total + rows_ref[d].astype(f32)
    norm_row = norm_row_ref[...].astype(f32)[0:1, :]
    total = jnp.where(iota((chunk, model), 0) == chunk - 1, norm_row, total).astype(bf16)
    for d in range(groups):
        out_ref[d] = total


def unpack_kernel(
    rows_ref, norm1_ref, wq_ref, wk_ref, wv_ref, wo_ref, bias_ref, norm2_ref, router_ref, all_ref
):
    groups, chunk, _ = rows_ref.shape
    inner = wo_ref.shape[0]
    experts = router_ref.shape[0]
    heads, buckets = bias_ref.shape
    count = 4 * inner // groups
    share = experts // groups
    norm1 = None
    for d in range(groups):
        all_ref[d * count : (d + 1) * count, :] = rows_ref[d, 0:count, :].astype(f32)
        tail = rows_ref[d, chunk - 16 : chunk, :].astype(f32)
        router_ref[d * share : (d + 1) * share, :] = tail[0:share, :]
        if d < heads:
            bias_ref[d : d + 1, :] = tail[8:9, 0:buckets]
        if d == 7:
            norm2_ref[...] = tail[8:9, :].reshape(norm2_ref.shape)
        norm1 = tail[15:16, :] if norm1 is None else norm1 + tail[15:16, :]
    norm1_ref[...] = norm1.reshape(norm1_ref.shape)
    for j, out in enumerate((wq_ref, wk_ref, wv_ref, wo_ref)):
        out[...] = all_ref[j * inner : (j + 1) * inner, :]


def layer_out_kernel(core_ref, y0_ref, y1_ref, y2_ref, y3_ref, hidden_ref, out_ref):
    width = y0_ref.shape[1]
    core = core_ref[0]
    own = half(None, core, width)
    oth = half(None, 1 - core, width)
    out_ref[:, own] = (
        hidden_ref[:, own] + (y0_ref[...].astype(f32) + y2_ref[...].astype(f32))
    ).astype(bf16)
    out_ref[:, oth] = (
        hidden_ref[:, oth] + (y1_ref[...].astype(f32) + y3_ref[...].astype(f32))
    ).astype(bf16)


def struct(shape, dtype):
    return jax.ShapeDtypeStruct(shape, dtype)


def body(
    groups,
    lanes,
    tokens,
    lengths,
    routes,
    rel_bucket,
    norm1,
    w_query,
    w_key,
    w_value,
    output_weight,
    position_bias_table,
    norm2,
    router,
    expert_in,
    expert_out,
    cotangent,
):
    span, model = tokens.shape
    heads, buckets = position_bias_table.shape
    inner = w_query.shape[1]
    experts = router.shape[1]
    local_experts, _, hidden_units = expert_in.shape
    capacity = 2 * routes.shape[1] * span // experts
    rows = local_experts * capacity
    width = model // 2
    rel_bucket = rel_bucket.reshape(1, -1)
    member = lax.axis_index("tensor")
    group = lax.axis_index("dp")
    halves = 2 if local_experts % 2 == 0 else 1
    far = member // 2
    place = jnp.stack([lax.rem(member, 2), group * local_experts, far, far * (halves - 1)])
    place = place.astype(jnp.int32)
    share = local_experts // halves
    sent = rows // halves

    def swap(value, bits):
        return lax.ppermute(value, "tensor", [(i, i ^ bits) for i in range(lanes)])

    def spread(value):
        far = swap(value, 2)
        return value, swap(value, 1), far, swap(far, 1)

    def exchange(value):
        return lax.all_to_all(value, "dp", split_axis=0, concat_axis=0, tiled=True)

    def add_low(left, right):
        return (left.astype(f32) + right.astype(f32)).astype(bf16)

    placing, grad_payload = call(
        functools.partial(route_kernel, experts=experts, capacity=capacity),
        (
            struct((experts * capacity, span), bf16),
            struct((groups, sent + 16, width), bf16),
        ),
        (place, routes.T, cotangent),
        [SMEM, VMEM, VMEM],
        3 * 10**9,
        6 * 10**6,
    )
    g_rows = [exchange(grad_payload)]
    output_weights = spread(output_weight)
    attended, q, k, v, probs = call(
        attention_kernel,
        (
            struct((span, inner), bf16),
            struct((span, inner), bf16),
            struct((span, inner), bf16),
            struct((span, inner), bf16),
            struct((heads, span, span), bf16),
        ),
        (lengths, tokens, rel_bucket, norm1, w_query.T, w_key.T, w_value.T, position_bias_table),
        [SMEM] + [VMEM] * 7,
        6 * 10**9,
        8 * 10**6,
    )
    attended_all = spread(attended)
    hidden, *payloads = call(
        hidden_kernel,
        (struct((span, model), f32),) + (struct((groups, sent, width), bf16),) * halves,
        (place, tokens) + attended_all + output_weights + (norm2, placing),
        [SMEM] + [VMEM] * 11,
        2 * 10**9,
        8 * 10**6,
        scratch_shapes=[
            pltpu.VMEM((span, model), bf16),
            pltpu.VMEM((4, span, inner), bf16),
            pltpu.VMEM((4, inner, model), bf16),
        ],
    )
    payloads[0], g_rows[0] = lax.optimization_barrier((payloads[0], g_rows[0]))
    if halves == 2:
        g_rows.append(swap(g_rows[0], 2))
    n_owns = [exchange(payloads[0])]

    blocks = min(groups, 8)
    steps = groups // blocks
    block_rows = blocks * capacity
    row_spec = pl.BlockSpec((blocks, capacity, width), lambda e, j, p: (j, e, 0))

    ids_spec = pl.BlockSpec((blocks, 16, width), lambda e, j, p: (j, sent // 16, 0))

    def kept_spec(columns):
        return pl.BlockSpec((1, block_rows, columns), lambda e, j, p: (e, j, 0))

    def ordered(e, p):
        return (p[3] ^ (e // share)) * share + lax.rem(e, share)

    in_spec = pl.BlockSpec((1, model, hidden_units), lambda e, j, p: (ordered(e, p), 0, 0))
    out_spec = pl.BlockSpec((1, hidden_units, model), lambda e, j, p: (ordered(e, p), 0, 0))
    router_spec = pl.BlockSpec((experts, model), lambda e, j, p: (0, 0))
    unit = 2 * groups * rows * model * hidden_units

    def expert_call(kernel, out_shape, operands, in_specs, out_specs, flops, nbytes, grid=None):
        return pl.pallas_call(
            kernel,
            out_shape=out_shape,
            grid_spec=pltpu.PrefetchScalarGridSpec(
                num_scalar_prefetch=1,
                grid=grid or (local_experts, steps),
                in_specs=in_specs,
                out_specs=out_specs,
            ),
            compiler_params=pltpu.CompilerParams(vmem_limit_bytes=expert_vmem_bytes),
            cost_estimate=pl.CostEstimate(flops=flops, bytes_accessed=nbytes, transcendentals=0),
        )(place, *operands)

    which = range(halves)
    n_oths = [None] * halves
    back_rows, y_rows, kept = [None] * halves, [None] * halves, [None] * halves
    part_struct = struct((groups, sent, width), bf16)

    def weight_spec(weight, part):
        return pl.BlockSpec((1,) + weight.shape[1:], lambda e, j, p: ((p[3] ^ part) * share + e, 0, 0))

    def part_kept(columns):
        return struct((share, groups * capacity, columns), bf16)

    def multiply_cotangent(part):
        g_own = g_rows[part]
        return expert_call(
            functools.partial(cotangent_kernel, part=part, share=share),
            (part_kept(hidden_units), part_kept(model), part_kept(experts)),
            (g_own, g_own, swap(g_own, 1), expert_out),
            [ids_spec, row_spec, row_spec, weight_spec(expert_out, part)],
            (kept_spec(hidden_units), kept_spec(model), kept_spec(experts)),
            unit // halves,
            20 * 10**6 // halves,
            grid=(share, steps),
        )

    backs = [multiply_cotangent(0)] + [None] * (halves - 1)
    if halves == 2:
        later, n_owns[0], back = lax.optimization_barrier((payloads[1], n_owns[0], backs[0][0]))
        backs[0] = (back,) + tuple(backs[0][1:])
        n_owns.append(exchange(later))
    for part in which:
        back, g_full, other = backs[part]
        n_oths[part] = swap(n_owns[part], 1)
        if part + 1 < halves:
            n_oths[part], g_rows[1] = lax.optimization_barrier((n_oths[part], g_rows[1]))
            backs[1] = multiply_cotangent(1)
        keep, send, act, grad_pre, y_keep, y_send, coefficient = expert_call(
            functools.partial(expert_grad_kernel, part=part, share=share),
            (part_struct, part_struct, part_kept(hidden_units), part_kept(hidden_units))
            + (part_struct, part_struct, part_kept(experts)),
            (n_owns[part], n_oths[part], back, other, router.T, expert_in, expert_out),
            [row_spec, row_spec, kept_spec(hidden_units), kept_spec(experts), router_spec]
            + [weight_spec(expert_in, part), weight_spec(expert_out, part)],
            (row_spec, row_spec, kept_spec(hidden_units), kept_spec(hidden_units))
            + (row_spec, row_spec, kept_spec(experts)),
            3 * unit // halves,
            35 * 10**6 // halves,
            grid=(share, steps),
        )
        kept[part] = (n_owns[part], n_oths[part], act, grad_pre, g_full, coefficient)
        total = add_low(keep, swap(send, 1))
        if part + 1 < halves:
            total, n_owns[1], other = lax.optimization_barrier((total, n_owns[1], backs[1][2]))
            backs[1] = tuple(backs[1][:2]) + (other,)
        elif part > 0:
            total, back_rows[0] = lax.optimization_barrier((total, back_rows[0]))
        total, y_send = lax.optimization_barrier((total, y_send))
        back_rows[part] = exchange(total)
        y_rows[part] = (y_keep, y_send)
    y_rows = [add_low(y_keep, swap(y_send, 1)) for y_keep, y_send in y_rows]
    last, y_rows[-1] = lax.optimization_barrier((kept[-1][5], y_rows[-1]))
    kept[-1] = kept[-1][:5] + (last,)
    if halves == 2:
        y_near, y_far = y_rows[0], swap(y_rows[1], 2)
    def combine(value, part, before=None, dtype=bf16, extra=None):
        parted = placing.reshape(groups, halves, sent, span)
        below = 0 if extra is None else 2 * experts
        before_spec = pl.BlockSpec((span, width), lambda i, p: (0, 0))
        extra_spec = pl.BlockSpec((experts, model), lambda i, p: (0, 0))
        placing_spec = pl.BlockSpec(
            (groups, 1, sent, span), lambda i, p: (0, p[3] ^ part, 0, 0)
        )
        rows_spec = pl.BlockSpec((groups, sent, width), lambda i, p: (0, 0, 0))
        return pl.pallas_call(
            functools.partial(combine_kernel, before=int(before is not None)),
            out_shape=struct((span + below, width), dtype),
            grid_spec=pltpu.PrefetchScalarGridSpec(
                num_scalar_prefetch=1,
                grid=(1,),
                in_specs=[placing_spec, rows_spec]
                + [before_spec] * (before is not None)
                + [extra_spec] * (extra is not None),
                out_specs=pl.BlockSpec((span + below, width), lambda i, p: (0, 0)),
            ),
            compiler_params=pltpu.CompilerParams(vmem_limit_bytes=vmem_bytes),
            cost_estimate=pl.CostEstimate(flops=10**9, bytes_accessed=4 * 10**6, transcendentals=0),
        )(place, parted, value, *(operand for operand in (before, extra) if operand is not None))

    grad_router = call(
        router_kernel,
        struct((experts, model), f32),
        (place,) + sum([(a, b, c) for a, b, _, _, _, c in kept], ()),
        [SMEM] + [VMEM] * (3 * halves),
        10**9,
        4 * 10**6,
    )
    before = None
    if halves == 2:
        before = combine(back_rows[0], 0, None, f32)
        grad_router, before = lax.optimization_barrier((grad_router, before))


    if halves == 2:
        back_rows[1], before = lax.optimization_barrier((back_rows[1], before))
        z = combine(back_rows[1], 1, before, bf16, grad_router)
        z, y_far = lax.optimization_barrier((z, y_far))
        y_rows = add_low(y_near, y_far)
    else:
        z = combine(back_rows[0], 0, None, bf16, grad_router)
        y_rows = y_rows[0]
    y_rows = exchange(y_rows)
    z = spread(z)
    chunk = -(-4 * inner // (16 * groups)) * 16 + 16
    grad_hidden, weights, low = call(
        attention_back_kernel,
        (
            struct((span, model), f32),
            struct((groups, chunk, model), bf16),
            struct((3, span, inner), bf16),
        ),
        (place,)
        + z
        + (hidden, cotangent, tokens, norm1, norm2, output_weight)
        + (attended, q, k, v, probs, rel_bucket),
        [SMEM] + [VMEM] * 16,
        4600 * 10**6,
        12 * 10**6,
        scratch_shapes=[pltpu.VMEM((span, model), f32), pltpu.VMEM((4 * inner, model), f32)],
    )
    weights, y_rows = lax.optimization_barrier((weights, y_rows))
    weight_rows = exchange(weights)
    piece_keep, piece_send = call(
        input_back_kernel,
        (struct((span, width), f32), struct((span, width), bf16)),
        (place, low, w_query.T, w_key.T, w_value.T),
        [SMEM] + [VMEM] * 4,
        10**9,
        4 * 10**6,
        scratch_shapes=[pltpu.VMEM((span, model), f32)],
    )
    piece = add_low(piece_keep, swap(piece_send, 1))
    grad_tokens, norm_row = call(
        finish_kernel,
        (struct((span, model), f32), struct((16, model), bf16)),
        (place,) + spread(piece) + (grad_hidden, tokens, norm1),
        [SMEM] + [VMEM] * 7,
        10**7,
        6 * 10**6,
        scratch_shapes=[pltpu.VMEM((span, model), f32)],
    )
    grad_pre, norm_row = lax.optimization_barrier((grad_pre, norm_row))
    operands, specs = (), []
    for part in which:
        if part == halves - 1:
            kept[part] = kept[part][:3] + (grad_pre,) + kept[part][4:]

        def near_index(e, first=part * share):
            return jnp.clip(e - first, 0, share - 1)

        operands = operands + kept[part][:5]
        for _ in range(2):
            specs.append(
                pl.BlockSpec((blocks, capacity, width), lambda e, j, p, f=near_index: (j, f(e), 0))
            )
        for columns in (hidden_units, hidden_units, model):
            specs.append(
                pl.BlockSpec((1, block_rows, columns), lambda e, j, p, f=near_index: (f(e), j, 0))
            )
    grad_expert_in, grad_expert_out = expert_call(
        functools.partial(expert_weight_kernel, share=share),
        (struct(expert_in.shape, f32), struct(expert_out.shape, f32)),
        operands,
        specs,
        (in_spec, out_spec),
        2 * unit,
        55 * 10**6,
    )
    norm_row, y_rows = lax.optimization_barrier((norm_row, y_rows))
    y_part = combine(y_rows, 0)
    weight_rows, y_part = lax.optimization_barrier((weight_rows, y_part))
    weight_rows = exchange(
        call(
            chunk_kernel,
            struct((groups, chunk, model), bf16),
            (weight_rows, norm_row),
            [VMEM] * 2,
            10**7,
            3 * 10**6,
        )
    )
    grad_norm1, grad_query, grad_key, grad_value, grad_output, grad_bias, grad_norm2, grad_router = call(
        unpack_kernel,
        (
            struct((model,), f32),
            struct((inner, model), f32),
            struct((inner, model), f32),
            struct((inner, model), f32),
            struct((inner, model), f32),
            struct((heads, buckets), f32),
            struct((model,), f32),
            struct((experts, model), f32),
        ),
        (weight_rows,),
        [VMEM],
        10**7,
        5 * 10**6,
        scratch_shapes=[pltpu.VMEM((4 * inner, model), f32)],
    )
    layer_out = call(
        layer_out_kernel,
        struct((span, model), bf16),
        (place,) + spread(y_part) + (hidden,),
        [SMEM] + [VMEM] * 5,
        10**7,
        4 * 10**6,
    )
    return (
        layer_out,
        grad_tokens,
        grad_norm1,
        grad_query.T,
        grad_key.T,
        grad_value.T,
        grad_output,
        grad_bias,
        grad_norm2,
        grad_router.T,
        grad_expert_in,
        grad_expert_out,
    )


def solution(mesh):
    in_specs = (
        P("dp", None),
        P("dp", None),
        P("dp", None),
        P(),
        P(),
        P(None, "tensor"),
        P(None, "tensor"),
        P(None, "tensor"),
        P("tensor", None),
        P("tensor", None),
        P(),
        P(),
        P("dp", None, "tensor"),
        P("dp", "tensor", None),
        P("dp", None),
    )
    out_specs = (
        P("dp", None),
        P("dp", None),
        P(),
        P(None, "tensor"),
        P(None, "tensor"),
        P(None, "tensor"),
        P("tensor", None),
        P("tensor", None),
        P(),
        P(),
        P("dp", None, "tensor"),
        P("dp", "tensor", None),
    )
    return jax.shard_map(
        functools.partial(body, mesh.shape["dp"], mesh.shape["tensor"]),
        mesh=mesh,
        in_specs=in_specs,
        out_specs=out_specs,
        check_vma=False,
    )
```
